256 devices in a mesh: expert: 16 (over z, y_hi), hrow: 8 (over x, core), hcol: 2 (over y_lo).
Axes of the slice: x: 4, y: 4 (y_hi: 2, y_lo: 2; y = y_hi * 2 + y_lo), z: 8, core: 2. Of those that a mesh axis runs over, the one named last changes fastest.
Arguments:
- tokens: bfloat16 [2048, 7168], P(('expert', 'hrow'), 'hcol')
- expert_ids: int32 [2048, 8], P(('expert', 'hrow')), may hold values from 0 to 127, all different within a row; in each aligned block of 16 rows (0 to 15, 16 to 31, ...) at most 2 rows name the same one
- weight: bfloat16 [128, 256, 7168], P(('expert', 'hrow'), None, 'hcol'), may hold values from -6 to 6
- mask_bits: int32 [256, 224], P(None, 'hcol'), may hold values from -2147483648 to 2147483646, as said below
- damping: float32 [128, 7168], P(('expert', 'hrow'), 'hcol'), may hold values from 0.5 to 2
Outputs:
- new_weight: bfloat16 [128, 256, 7168], P(('expert', 'hrow'), None, 'hcol')
The draws below stay inside these ranges and needn't reach their ends.
Inputs may be any that keep to these rules, and one draw needn't show every extreme that they name: `expert_ids`: each token names 8 different experts; among the 16 rows of one device (aligned blocks of rows) no expert is named more than 2 times, a bound that some block reaches. `mask_bits`: every bit of every word is a keep flag (1 keeps the entry, 0 prunes it).
All inputs are finite; a program needn't handle non-finite values.
Results may differ from the reference program's by a relative error of at most 0.0044.
Values may be sent and summed in bfloat16 or wider, within the bound.
No kernel may reach another device: no remote copies, remote signals or barrier semaphores. Data moves between devices by JAX's collectives and lax.ppermute only.
A program may use at most 64 MiB of HBM per device.

```python
import math
import jax
import jax.numpy as jnp
import numpy as np
from jax import lax

HD = 7168
TOPK = 8
SLAB = 256
EXP_DEV = 1
TOK_DEV = 16
EXPERTS = 128
TOKENS = 2048
CAP = 2
ROWS_E = 128


def draw_tokens(key, part):
    key_base = jax.random.fold_in(key, 11)
    key_rows = jax.random.fold_in(key, 12)
    key_cols = jax.random.fold_in(key, 13)
    base = jax.random.truncated_normal(key_base, -4.0, 4.0, (TOKENS, HD), jnp.float32)
    row_scale = jnp.exp(jax.random.uniform(key_rows, (TOKENS, 1), jnp.float32, math.log(0.5), math.log(1.6)))
    col_scale = jnp.exp(jax.random.uniform(key_cols, (1, HD), jnp.float32, math.log(0.5), math.log(1.6)))
    return (base * row_scale * col_scale).astype(jnp.bfloat16)


def draw_mask_bits(key, part):
    return jax.random.randint(jax.random.fold_in(key, 21), (SLAB, HD // 32), -2147483648, 2147483647, jnp.int32)


def shard_levels(own_key, dims, split, smallest, largest):
    level = 1.0
    for position, parts in split:
        heights = jax.random.uniform(jax.random.fold_in(jax.random.fold_in(own_key, 6), position), (parts,), jnp.float32, smallest / len(split), largest / len(split))
        level = level * jnp.repeat(jnp.exp(heights), dims[position] // parts).reshape((-1,) + (1,) * (len(dims) - 1 - position))
    return level


def shared_out(rng, own, number, rows, count, top, reach, slope):
    ranking = jax.random.permutation(rng, count)
    packed, ordinary = shares(count, rows * top, reach, slope, True), shares(count, rows * top, reach, slope, False)
    places = jnp.arange(count)

    def named(lengths, offset_by):
        used = int((lengths > 0).sum())
        fixed = max(1, used // 4)
        passed = fixed + (places - fixed + offset_by * (used - fixed)) % max(1, count - fixed)
        return jnp.zeros((count,), jnp.int32).at[ranking[jnp.where(places < fixed, places, passed)]].set(jnp.asarray(lengths, jnp.int32))

    lengths = jnp.where(number % 4 == 0, named(packed, number // 4), named(ordinary, number - number // 4 - 1))
    mixed = jax.random.permutation(jax.random.fold_in(own, 3), count)
    giver, sink = mixed[0:count // 2 * 2:2], mixed[1:count // 2 * 2:2]
    room = jnp.minimum(lengths[giver] - 1, reach - lengths[sink]) // 2
    room = jnp.where((giver == ranking[0]) | (sink == ranking[0]) | (lengths[sink] == 0), 0, jnp.maximum(room, 0))
    passed = jax.random.randint(jax.random.fold_in(own, 4), (count // 2,), 0, 1 << 20) % (room + 1)
    lengths = lengths.at[giver].add(-passed).at[sink].add(passed)
    labels = jnp.searchsorted(jnp.cumsum(lengths), jnp.arange(rows * top), side="right").astype(jnp.int32)
    grid = labels.reshape(top, rows).T
    grid = grid[jax.random.permutation(jax.random.fold_in(own, 1), rows)]
    offset_by = jax.random.randint(jax.random.fold_in(own, 2), (rows, 1), 0, top)
    return jnp.take_along_axis(grid, (jnp.arange(top)[None, :] + offset_by) % top, axis=1)


def shares(number_of, total, reach, skew, full):
    weights = [(1 << 20) // math.isqrt(grade ** skew) + 1 for grade in range(1, number_of + 1)]
    largest = reach if full else min(reach, max(-(-total // number_of), total * weights[0] // sum(weights)))
    least = 1 if total - largest >= number_of - 1 else 0
    given, surplus = [largest] + [least] * (number_of - 1), total - largest - least * (number_of - 1)
    while surplus > 0:
        free = [i for i in range(1, number_of) if given[i] < largest] or [i for i in range(1, number_of) if given[i] < reach]
        pool, left = sum([weights[i] for i in free]), surplus
        for i in free:
            more = min(reach - given[i], max(1, left * weights[i] // pool), surplus)
            given[i] = given[i] + more
            surplus = surplus - more
    return np.array(given)


def gaussian(stream_key, extent, spread, limit, split=(), kind=jnp.bfloat16):
    result = spread * jax.random.normal(stream_key, extent, jnp.float32)
    if split:
        result = result * shard_levels(stream_key, extent, split, -0.22, 0.18)
    return jnp.clip(result, -limit, limit).astype(kind)


def setup_inputs(seed: int = 0) -> dict:
    arg_keys = jax.random.split(jax.random.key(seed), 6)
    tokens = draw_tokens(jax.random.fold_in(arg_keys[5], 71), 0)
    expert_ids_keys = jax.random.split(jax.random.fold_in(arg_keys[1], 1), TOKENS // TOK_DEV)
    expert_ids_turns = jax.random.permutation(jax.random.fold_in(arg_keys[1], 3), TOKENS // TOK_DEV)
    expert_ids = jax.vmap(lambda own, number: shared_out(jax.random.fold_in(arg_keys[1], 2), own, number, TOK_DEV, EXPERTS, TOPK, CAP, 2))(expert_ids_keys, expert_ids_turns).reshape((TOKENS, TOPK))
    weight = gaussian(arg_keys[2], (EXPERTS, SLAB, HD), 1.0, 6.0, ((0, 128), (2, 2)))
    mask_bits = draw_mask_bits(jax.random.fold_in(arg_keys[5], 71), 0)
    damping = jnp.clip(jnp.exp(math.log(2.0) - 1.3862944 * jax.random.uniform(arg_keys[4], (EXPERTS, HD), jnp.float32) ** shard_levels(arg_keys[4], (EXPERTS, HD), ((0, 128), (1, 2)), -0.2, 0.2)), 0.5, 2.0)
    return {"tokens": tokens, "expert_ids": expert_ids, "weight": weight, "mask_bits": mask_bits, "damping": damping}


ETA = 0.5


def unpack_bits(bits):
    bit_shifts = jnp.arange(32, dtype=jnp.int32)
    bit_flags = jnp.bitwise_and(jnp.right_shift(bits[:, :, None], bit_shifts[None, None, :]), 1)
    return bit_flags.reshape(bits.shape[0], bits.shape[1] * 32)


def reference(tokens, expert_ids, weight, mask_bits, damping):
    keep_flags = unpack_bits(mask_bits)
    max_rows = (EXPERTS // EXP_DEV) * CAP

    def one_expert(inputs):
        expert, slab, lam_row = inputs
        member = jnp.any(expert_ids == expert, axis=1)
        picked = jnp.nonzero(member, size=max_rows, fill_value=0)[0].astype(jnp.int32)
        live_count = jnp.sum(member.astype(jnp.int32))
        valid = (jnp.arange(max_rows, dtype=jnp.int32) < live_count).astype(jnp.float32)
        routed = tokens[picked].astype(jnp.float32) * valid[:, None]
        pruned = jnp.where(keep_flags == 1, jnp.float32(0.0), slab.astype(jnp.float32))
        projected = lax.dot_general(pruned, routed, (((1,), (1,)), ((), ())), precision=lax.Precision.HIGHEST)
        projected = lax.optimization_barrier(projected.astype(jnp.bfloat16)).astype(jnp.float32)
        comp_term = jnp.dot(projected, routed, precision=lax.Precision.HIGHEST) / ROWS_E
        diag_scale = jnp.sum(routed * routed, axis=0) / ROWS_E + lam_row
        updated = slab.astype(jnp.float32) + ETA * comp_term / diag_scale[None, :]
        return jnp.where(keep_flags == 1, updated, jnp.float32(0.0)).astype(jnp.bfloat16)

    return lax.map(one_expert, (jnp.arange(EXPERTS, dtype=jnp.int32), weight, damping))
```

```python
import functools

import jax
import jax.numpy as jnp
from jax import lax
from jax.experimental import pallas as pl
from jax.experimental.pallas import tpu as pltpu
from jax.sharding import Mesh, PartitionSpec as P

ROWS_E = 128
ETA = 0.5
CAP = 2
LANES = 128
F32 = jnp.float32
BF16 = jnp.bfloat16


def call(body, out_shape, operands, flops, scratch=(), name=None):
    size = sum(o.size * o.dtype.itemsize for o in operands)
    outs = jax.tree.leaves(out_shape)
    size += sum(o.size * o.dtype.itemsize for o in outs)
    return pl.pallas_call(
        body,
        out_shape=out_shape,
        in_specs=[pl.BlockSpec(memory_space=pltpu.VMEM)] * len(operands),
        out_specs=jax.tree.map(lambda _: pl.BlockSpec(memory_space=pltpu.VMEM), out_shape),
        scratch_shapes=list(scratch),
        cost_estimate=pl.CostEstimate(flops=flops, bytes_accessed=size, transcendentals=0),
        compiler_params=pltpu.CompilerParams(vmem_limit_bytes=40 * 2**20),
        name=name,
    )(*operands)


def tag_body(tokens_ref, ids_ref, out_ref):
    rows, feats = tokens_ref.shape
    top = ids_ref.shape[0]
    out_ref[:, :feats] = tokens_ref[...]
    spread = (
        lax.broadcasted_iota(jnp.int32, (top, LANES), 0)
        == lax.broadcasted_iota(jnp.int32, (top, LANES), 1)
    ).astype(BF16)
    ids = ids_ref[...].astype(F32).astype(BF16)
    out_ref[:, feats:] = lax.dot_general(
        ids, spread, (((0,), (0,)), ((), ())), preferred_element_type=F32
    ).astype(BF16)


def pack_body(tok_rows, top, first_ref, *refs):
    *block_refs, out_ref, held = refs
    feats = out_ref.shape[-1]
    at = 0
    for ref in block_refs:
        held[at : at + ref.shape[0], :] = ref[...]
        at += ref.shape[0]
    tokens = at
    dests, per_dest = out_ref.shape[0], out_ref.shape[1]
    rows = dests * per_dest
    pick = (
        lax.broadcasted_iota(jnp.int32, (top, LANES), 0)
        == lax.broadcasted_iota(jnp.int32, (top, LANES), 1)
    ).astype(BF16)
    ids = lax.dot_general(
        pick, held[:, feats:], (((1,), (1,)), ((), ())), preferred_element_type=F32
    )
    row = lax.broadcasted_iota(jnp.int32, (rows, 1), 0)
    expert = (first_ref[0] + 2 * (row // per_dest)).astype(F32)
    block = (row % per_dest) // CAP
    slot = (row % CAP).astype(F32)
    tok = lax.broadcasted_iota(jnp.int32, (1, tokens), 1)
    named = ids[0:1, :] == expert
    for k in range(1, top):
        named = named | (ids[k : k + 1, :] == expert)
    named = named & (tok // tok_rows == block)
    member = jnp.where(named, 1.0, 0.0)
    before = (
        lax.broadcasted_iota(jnp.int32, (tokens, tokens), 0)
        < lax.broadcasted_iota(jnp.int32, (tokens, tokens), 1)
    ).astype(BF16)
    rank = jnp.dot(member.astype(BF16), before, preferred_element_type=F32)
    select = jnp.where(rank == slot, member, 0.0).astype(BF16)
    width = 512
    for lo in range(0, feats, width):
        out_ref[:, :, lo : lo + width] = (
            jnp.dot(select, held[:, lo : lo + width], preferred_element_type=F32)
            .astype(BF16)
            .reshape(dests, per_dest, width)
        )


def prune_body(weight_ref, bits_ref, pruned_ref, keep_ref):
    rows, words = bits_ref.shape
    feats = weight_ref.shape[1]
    lane = lax.broadcasted_iota(jnp.int32, (rows, LANES), 1)
    bits = jnp.concatenate([bits_ref[...], jnp.zeros((rows, LANES - words), jnp.int32)], axis=1)
    for j in range(feats // LANES):
        word = jnp.take_along_axis(bits, lane // 32 + 4 * j, axis=1, mode="promise_in_bounds")
        keep = jnp.bitwise_and(jnp.right_shift(word, lane % 32), 1).astype(F32)
        cols = slice(j * LANES, (j + 1) * LANES)
        slab = weight_ref[:, cols].astype(F32)
        pruned_ref[:, cols] = jnp.where(keep > 0.5, 0.0, slab).astype(BF16)
        keep_ref[:, cols] = keep.astype(BF16)


def project_body(routed_ref, pruned_ref, part_ref, low_ref):
    part = lax.dot_general(
        routed_ref[...], pruned_ref[...], (((1,), (1,)), ((), ())), preferred_element_type=F32
    )
    part_ref[...] = part
    low_ref[...] = part.astype(BF16)


def scale_body(routed_ref, damping_ref, scale_ref):
    feats = routed_ref.shape[1]
    width = 512
    for lo in range(0, feats, width):
        cols = slice(lo, lo + width)
        rows = routed_ref[:, cols].astype(F32)
        diag = jnp.sum(rows * rows, axis=0, keepdims=True) * (1.0 / ROWS_E) + damping_ref[:, cols]
        scale_ref[:, cols] = (ETA / ROWS_E) / diag


def update_body(part_ref, other_ref, routed_ref, scale_ref, weight_ref, keep_ref, out_ref):
    feats = routed_ref.shape[1]
    projected = (part_ref[...] + other_ref[...].astype(F32)).astype(BF16)
    width = 512
    for lo in range(0, feats, width):
        cols = slice(lo, lo + width)
        comp = lax.dot_general(
            projected, routed_ref[:, cols], (((0,), (0,)), ((), ())), preferred_element_type=F32
        )
        updated = weight_ref[:, cols].astype(F32) + comp * scale_ref[:, cols]
        out_ref[:, cols] = jnp.where(keep_ref[:, cols].astype(F32) > 0.5, updated, 0.0).astype(BF16)


def shape(*dims, dtype=BF16):
    return jax.ShapeDtypeStruct(dims, dtype)


def shift(x, axis, step):
    n = lax.axis_size(axis)
    return lax.ppermute(x, axis, [(i, (i + step) % n) for i in range(n)])


def local(tokens, expert_ids, weight, mask_bits, damping):
    tok_rows, feats = tokens.shape
    top = expert_ids.shape[1]
    slab = weight.shape[1]
    weight = weight.reshape(slab, feats)
    me_z, me_core = lax.axis_index("z"), lax.axis_index("core")
    plane = lax.axis_size("yh") * lax.axis_size("x")
    first = (me_z * plane * 2 + me_core).astype(jnp.int32).reshape(1)

    with jax.named_scope("tag"):
        own = call(tag_body, shape(tok_rows, feats + LANES), (tokens, expert_ids.T), 1 << 16)
    with jax.named_scope("gather_z"):
        m1, p1 = shift(own, "z", 1), shift(own, "z", -1)
        m2, p2 = shift(m1, "z", 1), shift(p1, "z", -1)
        m3, p3 = shift(m1, "z", 2), shift(p1, "z", -2)
        far = shift(m3, "z", 1)
    groups = ((own, m1, p1), (m2, p2, m3, p3), (far,))
    with jax.named_scope("swap_core"):
        swapped = tuple(shift(jnp.concatenate(g), "core", 1) for g in groups)
    blocks = tuple(b for g in groups for b in g) + swapped
    n_tok = sum(b.shape[0] for b in blocks)
    per_dest = n_tok // tok_rows * CAP
    with jax.named_scope("pack"):
        packed = pl.pallas_call(
            functools.partial(pack_body, tok_rows, top),
            out_shape=shape(plane, per_dest, feats),
            in_specs=[pl.BlockSpec(memory_space=pltpu.SMEM)]
            + [pl.BlockSpec(memory_space=pltpu.VMEM)] * len(blocks),
            out_specs=pl.BlockSpec(memory_space=pltpu.VMEM),
            scratch_shapes=[pltpu.VMEM((n_tok, feats + LANES), BF16)],
            cost_estimate=pl.CostEstimate(
                flops=2 * plane * per_dest * n_tok * feats, bytes_accessed=4 << 20, transcendentals=0
            ),
            compiler_params=pltpu.CompilerParams(vmem_limit_bytes=40 * 2**20),
        )(first, *blocks)
    with jax.named_scope("prune"):
        pruned, keep = call(
            prune_body, (shape(slab, feats), shape(slab, feats)), (weight, mask_bits), 1 << 22
        )
    with jax.named_scope("route"):
        block = lax.all_to_all(packed, ("yh", "x"), split_axis=0, concat_axis=0, tiled=True)
    routed = block.reshape(plane * per_dest, feats)
    rows = routed.shape[0]
    with jax.named_scope("project"):
        part, low = call(
            project_body,
            (shape(rows, slab, dtype=F32), shape(rows, slab)),
            (routed, pruned),
            2 * rows * slab * feats,
        )
    with jax.named_scope("swap_features"):
        other = shift(low, "yl", 1)
    with jax.named_scope("scale"):
        scale = call(scale_body, shape(1, feats, dtype=F32), (routed, damping), 2 * rows * feats)
    with jax.named_scope("update"):
        out = call(
            update_body,
            shape(slab, feats),
            (part, other, routed, scale, weight, keep),
            2 * rows * slab * feats,
        )
    return out.reshape(1, slab, feats)


def solution(mesh):
    n_hrow, n_hcol = mesh.shape["hrow"], mesh.shape["hcol"]
    n_expert = mesh.shape["expert"]
    fine = Mesh(
        mesh.devices.reshape(n_expert // 2, 2, n_hrow // 2, 2, n_hcol),
        ("z", "yh", "x", "core", "yl"),
    )
    own = ("z", "yh", "x", "core")
    in_specs = (P(own, "yl"), P(own, None), P(own, None, "yl"), P(None, "yl"), P(own, "yl"))
    return jax.shard_map(
        local, mesh=fine, in_specs=in_specs, out_specs=P(own, None, "yl"), check_vma=False
    )
```

```python
import functools

import jax
import jax.numpy as jnp
from jax import lax
from jax.experimental import pallas as pl
from jax.experimental.pallas import tpu as pltpu
from jax.sharding import Mesh, PartitionSpec as P

ROWS_E = 128
ETA = 0.5
CAP = 2
LANES = 128
WIDTH = 896
VMEM = 16 * 2**20
F32 = jnp.float32
BF16 = jnp.bfloat16


def call(body, out_shape, operands, flops, scratch=(), name=None):
    size = sum(o.size * o.dtype.itemsize for o in operands)
    outs = jax.tree.leaves(out_shape)
    size += sum(o.size * o.dtype.itemsize for o in outs)
    return pl.pallas_call(
        body,
        out_shape=out_shape,
        in_specs=[pl.BlockSpec(memory_space=pltpu.VMEM)] * len(operands),
        out_specs=jax.tree.map(lambda _: pl.BlockSpec(memory_space=pltpu.VMEM), out_shape),
        scratch_shapes=list(scratch),
        cost_estimate=pl.CostEstimate(flops=flops, bytes_accessed=size, transcendentals=0),
        compiler_params=pltpu.CompilerParams(vmem_limit_bytes=VMEM),
        name=name,
    )(*operands)


def tag_body(tokens_hbm, ids_hbm, out_ref, ids_ref, sems):
    feats = tokens_hbm.shape[1]
    top = ids_ref.shape[0]
    get_ids = pltpu.make_async_copy(ids_hbm, ids_ref, sems.at[0])
    get_tokens = pltpu.make_async_copy(tokens_hbm, out_ref.at[:, pl.ds(0, feats)], sems.at[1])
    get_ids.start()
    get_tokens.start()
    spread = (
        lax.broadcasted_iota(jnp.int32, (top, LANES), 0)
        == lax.broadcasted_iota(jnp.int32, (top, LANES), 1)
    ).astype(BF16)
    get_ids.wait()
    ids = ids_ref[...].astype(F32).astype(BF16)
    out_ref[:, feats:] = lax.dot_general(
        ids, spread, (((0,), (0,)), ((), ())), preferred_element_type=F32
    ).astype(BF16)
    get_tokens.wait()


def pack_body(tok_rows, top, first_ref, *refs):
    *block_refs, out_hbm, held, out_ref, sems = refs
    feats = out_ref.shape[-1]
    at = 0
    for ref in block_refs:
        held[at : at + ref.shape[0], :] = ref[...]
        at += ref.shape[0]
    tokens = at
    dests, per_dest = out_ref.shape[0], out_ref.shape[1]
    rows = dests * per_dest
    pick = (
        lax.broadcasted_iota(jnp.int32, (top, LANES), 0)
        == lax.broadcasted_iota(jnp.int32, (top, LANES), 1)
    ).astype(BF16)
    ids = lax.dot_general(
        pick, held[:, feats:], (((1,), (1,)), ((), ())), preferred_element_type=F32
    )
    row = lax.broadcasted_iota(jnp.int32, (rows, 1), 0)
    expert = (first_ref[0] + 2 * (row // per_dest)).astype(F32)
    block = (row % per_dest) // CAP
    slot = (row % CAP).astype(F32)
    tok = lax.broadcasted_iota(jnp.int32, (1, tokens), 1)
    named = ids[0:1, :] == expert
    for k in range(1, top):
        named = named | (ids[k : k + 1, :] == expert)
    named = named & (tok // tok_rows == block)
    member = jnp.where(named, 1.0, 0.0)
    before = (
        lax.broadcasted_iota(jnp.int32, (tokens, tokens), 0)
        < lax.broadcasted_iota(jnp.int32, (tokens, tokens), 1)
    ).astype(BF16)
    rank = jnp.dot(member.astype(BF16), before, preferred_element_type=F32)
    select = jnp.where(rank == slot, member, 0.0).astype(BF16)
    copies = []
    for i, lo in enumerate(range(0, feats, WIDTH)):
        out_ref[:, :, lo : lo + WIDTH] = (
            jnp.dot(select, held[:, lo : lo + WIDTH], preferred_element_type=F32)
            .astype(BF16)
            .reshape(dests, per_dest, WIDTH)
        )
        cols = (slice(None), slice(None), pl.ds(lo, WIDTH))
        copies.append(pltpu.make_async_copy(out_ref.at[cols], out_hbm.at[cols], sems.at[i]))
        copies[-1].start()
    for copy in copies:
        copy.wait()


def prune_body(weight_ref, bits_ref, pruned_ref, kept_ref, keep_ref):
    rows, words = bits_ref.shape
    feats = weight_ref.shape[1]
    lane = lax.broadcasted_iota(jnp.int32, (rows, LANES), 1)
    bits = jnp.concatenate([bits_ref[...], jnp.zeros((rows, LANES - words), jnp.int32)], axis=1)
    for j in range(feats // LANES):
        word = jnp.take_along_axis(bits, lane // 32 + 4 * j, axis=1, mode="promise_in_bounds")
        keep = jnp.bitwise_and(jnp.right_shift(word, lane % 32), 1).astype(F32)
        cols = slice(j * LANES, (j + 1) * LANES)
        slab = weight_ref[:, cols].astype(F32)
        pruned_ref[:, cols] = jnp.where(keep > 0.5, 0.0, slab).astype(BF16)
        kept_ref[:, cols] = jnp.where(keep > 0.5, slab, 0.0).astype(BF16)
        keep_ref[:, cols] = keep.astype(BF16)


def project_body(routed_ref, pruned_ref, part_ref, low_ref, routed_hbm=None, sem=None):
    if sem is not None:
        away = pltpu.make_async_copy(routed_ref, routed_hbm, sem)
        away.start()
    part = lax.dot_general(
        pruned_ref[...], routed_ref[...], (((1,), (1,)), ((), ())), preferred_element_type=F32
    )
    part_ref[...] = part
    low_ref[...] = part.astype(BF16)
    if sem is not None:
        away.wait()


def scale_body(*refs):
    *routed_refs, damping_ref, scale_ref = refs
    feats = damping_ref.shape[1]
    for lo in range(0, feats, WIDTH):
        cols = slice(lo, lo + WIDTH)
        diag = damping_ref[:, cols]
        for ref in routed_refs:
            rows = ref[:, cols].astype(F32)
            diag = diag + jnp.sum(rows * rows, axis=0, keepdims=True) * (1.0 / ROWS_E)
        scale_ref[:, cols] = (ETA / ROWS_E) / diag


def update_body(n, *refs):
    parts, others, routed_refs = refs[:n], refs[n : 2 * n], refs[2 * n : 3 * n]
    scale_ref, kept_ref, keep_ref, out_hbm, out_ref, sems = refs[3 * n :]
    feats = kept_ref.shape[1]
    projected = [(p[...] + o[...].astype(F32)).astype(BF16) for p, o in zip(parts, others)]
    copies = []
    for i, lo in enumerate(range(0, feats, WIDTH)):
        cols = slice(lo, lo + WIDTH)
        comp = jnp.dot(projected[0], routed_refs[0][:, cols], preferred_element_type=F32)
        for p, r in zip(projected[1:], routed_refs[1:]):
            comp = comp + jnp.dot(p, r[:, cols], preferred_element_type=F32)
        gain = keep_ref[:, cols].astype(F32) * (comp * scale_ref[:, cols])
        out_ref[:, cols] = (kept_ref[:, cols].astype(F32) + gain).astype(BF16)
        cols = (slice(None), pl.ds(lo, WIDTH))
        copies.append(pltpu.make_async_copy(out_ref.at[cols], out_hbm.at[cols], sems.at[i]))
        copies[-1].start()
    for copy in copies:
        copy.wait()


def shape(*dims, dtype=BF16):
    return jax.ShapeDtypeStruct(dims, dtype)


def shift(x, axis, step):
    n = lax.axis_size(axis)
    return lax.ppermute(x, axis, [(i, (i + step) % n) for i in range(n)])


def pack(first, blocks, tok_rows, top, feats, plane):
    n_tok = sum(b.shape[0] for b in blocks)
    per_dest = n_tok // tok_rows * CAP
    return pl.pallas_call(
        functools.partial(pack_body, tok_rows, top),
        out_shape=shape(plane, per_dest, feats),
        in_specs=[pl.BlockSpec(memory_space=pltpu.SMEM)]
        + [pl.BlockSpec(memory_space=pltpu.VMEM)] * len(blocks),
        out_specs=pl.BlockSpec(memory_space=pltpu.HBM),
        scratch_shapes=[
            pltpu.VMEM((n_tok, feats + LANES), BF16),
            pltpu.VMEM((plane, per_dest, feats), BF16),
            pltpu.SemaphoreType.DMA((feats // WIDTH,)),
        ],
        cost_estimate=pl.CostEstimate(
            flops=1, bytes_accessed=1, transcendentals=0
        ),
        compiler_params=pltpu.CompilerParams(vmem_limit_bytes=VMEM),
    )(first, *blocks)


def local(tokens, expert_ids, weight, mask_bits, damping):
    tok_rows, feats = tokens.shape
    top = expert_ids.shape[1]
    slab = weight.shape[1]
    weight = weight.reshape(slab, feats)
    me_z, me_core = lax.axis_index("z"), lax.axis_index("core")
    plane = lax.axis_size("yh") * lax.axis_size("x")
    first = (me_z * plane * 2 + me_core).astype(jnp.int32).reshape(1)
    hbm, vmem = pl.BlockSpec(memory_space=pltpu.HBM), pl.BlockSpec(memory_space=pltpu.VMEM)

    with jax.named_scope("tag"):
        own = pl.pallas_call(
            tag_body,
            out_shape=shape(tok_rows, feats + LANES),
            in_specs=[hbm, hbm],
            out_specs=vmem,
            scratch_shapes=[
                pltpu.VMEM((top, tok_rows), jnp.int32),
                pltpu.SemaphoreType.DMA((2,)),
            ],
            compiler_params=pltpu.CompilerParams(vmem_limit_bytes=VMEM),
        )(tokens, expert_ids.T)

    def packed(blocks):
        with jax.named_scope("pack"):
            return pack(first, blocks, tok_rows, top, feats, plane)

    def route(rows):
        with jax.named_scope("route"):
            block = lax.all_to_all(rows, ("yh", "x"), split_axis=0, concat_axis=0, tiled=True)
        return block.reshape(-1, feats)

    with jax.named_scope("gather_near"):
        m1, p1, m2 = shift(own, "z", 1), shift(own, "z", -1), shift(own, "z", 2)
    with jax.named_scope("gather_far"):
        p23 = shift(jnp.concatenate((own, p1)), "z", -2)
        m34 = shift(jnp.concatenate((m1, m2)), "z", 2)

    def swap(group):
        with jax.named_scope("swap_core"):
            return (*group, shift(jnp.concatenate(group), "core", 1))

    routed1 = route(packed(swap((own, m1, p1, m2))))
    routed2 = route(packed(swap((p23, m34))))
    with jax.named_scope("prune"):
        pruned, kept, keep = call(
            prune_body, (shape(slab, feats),) * 3, (weight, mask_bits), 1 << 22
        )

    def project(routed, away):
        rows = routed.shape[0]
        with jax.named_scope("project"):
            return pl.pallas_call(
                project_body,
                out_shape=(shape(slab, rows, dtype=F32), shape(slab, rows))
                + ((shape(rows, feats),) if away else ()),
                in_specs=[vmem, vmem],
                out_specs=(vmem, vmem) + ((hbm,) if away else ()),
                scratch_shapes=[pltpu.SemaphoreType.DMA] if away else [],
                cost_estimate=pl.CostEstimate(
                    flops=2 * rows * slab * feats, bytes_accessed=1 << 21, transcendentals=0
                ),
                compiler_params=pltpu.CompilerParams(vmem_limit_bytes=VMEM),
            )(routed, pruned)

    part1, low1, routed1 = project(routed1, True)
    with jax.named_scope("swap_features"):
        other1 = shift(low1, "yl", 1)
    part2, low2 = project(routed2, False)
    with jax.named_scope("swap_features"):
        other2 = shift(low2, "yl", 1)
    with jax.named_scope("scale"):
        scale = call(
            scale_body, shape(1, feats, dtype=F32), (routed1, routed2, damping), 4 * slab * feats
        )
    with jax.named_scope("update"):
        operands = (part1, part2, other1, other2, routed1, routed2, scale, kept, keep)
        out = pl.pallas_call(
            functools.partial(update_body, 2),
            out_shape=shape(slab, feats),
            in_specs=[vmem] * len(operands),
            out_specs=hbm,
            scratch_shapes=[
                pltpu.VMEM((slab, feats), BF16),
                pltpu.SemaphoreType.DMA((feats // WIDTH,)),
            ],
            compiler_params=pltpu.CompilerParams(vmem_limit_bytes=VMEM),
        )(*operands)
    return out.reshape(1, slab, feats)


def solution(mesh):
    n_hrow, n_hcol = mesh.shape["hrow"], mesh.shape["hcol"]
    n_expert = mesh.shape["expert"]
    fine = Mesh(
        mesh.devices.reshape(n_expert // 2, 2, n_hrow // 2, 2, n_hcol),
        ("z", "yh", "x", "core", "yl"),
    )
    own = ("z", "yh", "x", "core")
    in_specs = (P(own, "yl"), P(own, None), P(own, None, "yl"), P(None, "yl"), P(own, "yl"))
    return jax.shard_map(
        local, mesh=fine, in_specs=in_specs, out_specs=P(own, None, "yl"), check_vma=False
    )
```

```python
import functools

import jax
import jax.numpy as jnp
from jax import lax
from jax.experimental import pallas as pl
from jax.experimental.pallas import tpu as pltpu
from jax.sharding import Mesh, PartitionSpec as P

ROWS_E = 128
ETA = 0.5
CAP = 2
LANES = 128
WIDTH = 896
VMEM = 16 * 2**20
GATE = 4
F32 = jnp.float32
BF16 = jnp.bfloat16


def call(body, out_shape, operands, flops, scratch=(), name=None):
    size = sum(o.size * o.dtype.itemsize for o in operands)
    outs = jax.tree.leaves(out_shape)
    size += sum(o.size * o.dtype.itemsize for o in outs)
    return pl.pallas_call(
        body,
        out_shape=out_shape,
        in_specs=[pl.BlockSpec(memory_space=pltpu.VMEM)] * len(operands),
        out_specs=jax.tree.map(lambda _: pl.BlockSpec(memory_space=pltpu.VMEM), out_shape),
        scratch_shapes=list(scratch),
        cost_estimate=pl.CostEstimate(flops=flops, bytes_accessed=size, transcendentals=0),
        compiler_params=pltpu.CompilerParams(vmem_limit_bytes=VMEM),
        name=name,
    )(*operands)


def tag_body(tokens_hbm, ids_hbm, out_ref, ids_ref, sems):
    feats = tokens_hbm.shape[1]
    top = ids_ref.shape[0]
    get_ids = pltpu.make_async_copy(ids_hbm, ids_ref, sems.at[0])
    get_tokens = pltpu.make_async_copy(tokens_hbm, out_ref.at[:, pl.ds(0, feats)], sems.at[1])
    get_ids.start()
    get_tokens.start()
    spread = (
        lax.broadcasted_iota(jnp.int32, (top, LANES), 0)
        == lax.broadcasted_iota(jnp.int32, (top, LANES), 1)
    ).astype(BF16)
    get_ids.wait()
    ids = ids_ref[...].astype(F32).astype(BF16)
    out_ref[:, feats:] = lax.dot_general(
        ids, spread, (((0,), (0,)), ((), ())), preferred_element_type=F32
    ).astype(BF16)
    get_tokens.wait()


def pack_body(tok_rows, top, n_in, experts_ref, *refs):
    block_refs, out_refs, held = refs[:n_in], refs[n_in:-1], refs[-1]
    feats = out_refs[0].shape[-1]
    at = 0
    for ref in block_refs:
        held[at : at + ref.shape[0], :] = ref[...]
        at += ref.shape[0]
    tokens = at
    dests, per_dest = len(out_refs), out_refs[0].shape[0]
    rows = dests * per_dest
    pick = (
        lax.broadcasted_iota(jnp.int32, (top, LANES), 0)
        == lax.broadcasted_iota(jnp.int32, (top, LANES), 1)
    ).astype(BF16)
    ids = lax.dot_general(
        pick, held[:, feats:], (((1,), (1,)), ((), ())), preferred_element_type=F32
    )
    row = lax.broadcasted_iota(jnp.int32, (rows, 1), 0)
    expert = jnp.zeros((rows, 1), jnp.int32)
    for j in range(dests):
        expert = jnp.where(row // per_dest == j, experts_ref[j], expert)
    expert = expert.astype(F32)
    block = (row % per_dest) // CAP
    slot = (row % CAP).astype(F32)
    tok = lax.broadcasted_iota(jnp.int32, (1, tokens), 1)
    named = ids[0:1, :] == expert
    for k in range(1, top):
        named = named | (ids[k : k + 1, :] == expert)
    named = named & (tok // tok_rows == block)
    member = jnp.where(named, 1.0, 0.0)
    before = (
        lax.broadcasted_iota(jnp.int32, (tokens, tokens), 0)
        < lax.broadcasted_iota(jnp.int32, (tokens, tokens), 1)
    ).astype(BF16)
    rank = jnp.dot(member.astype(BF16), before, preferred_element_type=F32)
    select = jnp.where(rank == slot, member, 0.0).astype(BF16)
    for lo in range(0, feats, WIDTH):
        cols = slice(lo, lo + WIDTH)
        picked = jnp.dot(select, held[:, cols], preferred_element_type=F32).astype(BF16)
        for j, ref in enumerate(out_refs):
            ref[:, cols] = picked[j * per_dest : (j + 1) * per_dest]


def prune_body(weight_ref, bits_ref, pruned_ref, kept_ref, keep_ref):
    rows, words = bits_ref.shape
    feats = weight_ref.shape[1]
    lane = lax.broadcasted_iota(jnp.int32, (rows, LANES), 1)
    bits = jnp.concatenate([bits_ref[...], jnp.zeros((rows, LANES - words), jnp.int32)], axis=1)
    for j in range(feats // LANES):
        word = jnp.take_along_axis(bits, lane // 32 + 4 * j, axis=1, mode="promise_in_bounds")
        keep = jnp.bitwise_and(jnp.right_shift(word, lane % 32), 1).astype(F32)
        cols = slice(j * LANES, (j + 1) * LANES)
        slab = weight_ref[:, cols].astype(F32)
        pruned_ref[:, cols] = jnp.where(keep > 0.5, 0.0, slab).astype(BF16)
        kept_ref[:, cols] = jnp.where(keep > 0.5, slab, 0.0).astype(BF16)
        keep_ref[:, cols] = keep.astype(BF16)


def project_body(n_in, *refs):
    blocks, pruned_ref, part_ref, low_ref, routed_ref = refs[:n_in], *refs[n_in:]
    at = 0
    for ref in blocks:
        routed_ref[at : at + ref.shape[0], :] = ref[...]
        at += ref.shape[0]
    part = lax.dot_general(
        pruned_ref[...], routed_ref[...], (((1,), (1,)), ((), ())), preferred_element_type=F32
    )
    part_ref[...] = part
    low_ref[...] = part.astype(BF16)


def scale_body(*refs):
    *routed_refs, damping_ref, scale_ref = refs
    feats = damping_ref.shape[1]
    for lo in range(0, feats, WIDTH):
        cols = slice(lo, lo + WIDTH)
        diag = damping_ref[:, cols]
        for ref in routed_refs:
            rows = ref[:, cols].astype(F32)
            diag = diag + jnp.sum(rows * rows, axis=0, keepdims=True) * (1.0 / ROWS_E)
        scale_ref[:, cols] = (ETA / ROWS_E) / diag


def update_body(n, *refs):
    parts, others, routed_refs = refs[:n], refs[n : 2 * n], refs[2 * n : 3 * n]
    scale_ref, kept_ref, keep_ref, out_hbm, out_ref, sems = refs[3 * n :]
    feats = kept_ref.shape[1]
    projected = [(p[...] + o[...].astype(F32)).astype(BF16) for p, o in zip(parts, others)]
    copies = []
    for i, lo in enumerate(range(0, feats, WIDTH)):
        cols = slice(lo, lo + WIDTH)
        comp = jnp.dot(projected[0], routed_refs[0][:, cols], preferred_element_type=F32)
        for p, r in zip(projected[1:], routed_refs[1:]):
            comp = comp + jnp.dot(p, r[:, cols], preferred_element_type=F32)
        gain = keep_ref[:, cols].astype(F32) * (comp * scale_ref[:, cols])
        out_ref[:, cols] = (kept_ref[:, cols].astype(F32) + gain).astype(BF16)
        cols = (slice(None), pl.ds(lo, WIDTH))
        copies.append(pltpu.make_async_copy(out_ref.at[cols], out_hbm.at[cols], sems.at[i]))
        copies[-1].start()
    for copy in copies:
        copy.wait()


def shape(*dims, dtype=BF16):
    return jax.ShapeDtypeStruct(dims, dtype)


def shift(x, axis, step):
    n = lax.axis_size(axis)
    return lax.ppermute(x, axis, [(i, (i + step) % n) for i in range(n)])


def pack(experts, blocks, tok_rows, top, feats, dests):
    n_tok = sum(b.shape[0] for b in blocks)
    per_dest = n_tok // tok_rows * CAP
    vmem = pl.BlockSpec(memory_space=pltpu.VMEM)
    return pl.pallas_call(
        functools.partial(pack_body, tok_rows, top, len(blocks)),
        out_shape=(shape(per_dest, feats),) * dests,
        in_specs=[pl.BlockSpec(memory_space=pltpu.SMEM)] + [vmem] * len(blocks),
        out_specs=(vmem,) * dests,
        scratch_shapes=[pltpu.VMEM((n_tok, feats + LANES), BF16)],
        cost_estimate=pl.CostEstimate(flops=1, bytes_accessed=1, transcendentals=0),
        compiler_params=pltpu.CompilerParams(vmem_limit_bytes=VMEM),
    )(experts, *blocks)


def after(x, *others):
    return lax.optimization_barrier((x, *others))[0]


def local(tokens, expert_ids, weight, mask_bits, damping):
    tok_rows, feats = tokens.shape
    top = expert_ids.shape[1]
    slab = weight.shape[1]
    weight = weight.reshape(slab, feats)
    n_yh, n_x = lax.axis_size("yh"), lax.axis_size("x")
    z, yh, x, core = (lax.axis_index(a) for a in ("z", "yh", "x", "core"))
    steps = sorted(
        ((dy, dx) for dy in range(n_yh) for dx in range(n_x)),
        key=lambda s: (s[0] + min(s[1], n_x - s[1]), s),
    )
    experts = jnp.stack(
        [
            ((z * n_yh + (yh + dy) % n_yh) * n_x + (x + dx) % n_x) * lax.axis_size("core") + core
            for dy, dx in steps
        ]
    ).astype(jnp.int32)

    def send(rows, step):
        dy, dx = step
        pairs = [
            (a * n_x + b, (a + dy) % n_yh * n_x + (b + dx) % n_x)
            for a in range(n_yh)
            for b in range(n_x)
        ]
        with jax.named_scope("route"):
            return lax.ppermute(rows, ("yh", "x"), pairs)

    hbm, vmem = pl.BlockSpec(memory_space=pltpu.HBM), pl.BlockSpec(memory_space=pltpu.VMEM)

    with jax.named_scope("tag"):
        own = pl.pallas_call(
            tag_body,
            out_shape=shape(tok_rows, feats + LANES),
            in_specs=[hbm, hbm],
            out_specs=vmem,
            scratch_shapes=[
                pltpu.VMEM((top, tok_rows), jnp.int32),
                pltpu.SemaphoreType.DMA((2,)),
            ],
            compiler_params=pltpu.CompilerParams(vmem_limit_bytes=VMEM),
        )(tokens, expert_ids.T)

    def packed(blocks):
        with jax.named_scope("pack"):
            return pack(experts, blocks, tok_rows, top, feats, len(steps))

    def swap(group):
        with jax.named_scope("swap_core"):
            return shift(group, "core", 1)

    with jax.named_scope("gather_near"):
        m1, p1, m2 = shift(own, "z", 1), shift(own, "z", -1), shift(own, "z", 2)
    with jax.named_scope("gather_far"):
        p23 = shift(after(jnp.concatenate((own, p1)), m1, m2), "z", -2)
        m34 = shift(jnp.concatenate((m1, m2)), "z", 2)
    near = (own, m1, p1, m2)
    rows1 = packed((*near, swap(jnp.concatenate(near))))
    got1 = [rows1[0]] + [send(r, s) for r, s in zip(rows1[1:], steps[1:])]
    far = after(jnp.concatenate((p23, m34)), *got1[1:GATE])
    rows2 = packed((p23, m34, swap(far)))
    got2 = [rows2[0]]
    for k, (r, s) in enumerate(zip(rows2[1:], steps[1:])):
        late = got1[GATE + k : GATE + k + 1]
        got2.append(send(after(r, *late) if late else r, s))
    with jax.named_scope("prune"):
        pruned, kept, keep = call(
            prune_body, (shape(slab, feats),) * 3, (weight, mask_bits), 1 << 22
        )

    def project(blocks):
        rows = sum(b.shape[0] for b in blocks)
        with jax.named_scope("project"):
            return pl.pallas_call(
                functools.partial(project_body, len(blocks)),
                out_shape=(shape(slab, rows, dtype=F32), shape(slab, rows), shape(rows, feats)),
                in_specs=[vmem] * (len(blocks) + 1),
                out_specs=(vmem,) * 3,
                cost_estimate=pl.CostEstimate(
                    flops=2 * rows * slab * feats, bytes_accessed=1 << 21, transcendentals=0
                ),
                compiler_params=pltpu.CompilerParams(vmem_limit_bytes=VMEM),
            )(*blocks, pruned)

    part1, low1, routed1 = project(got1)
    with jax.named_scope("swap_features"):
        other1 = shift(low1, "yl", 1)
    part2, low2, routed2 = project(got2)
    with jax.named_scope("swap_features"):
        other2 = shift(low2, "yl", 1)
    with jax.named_scope("scale"):
        scale = call(
            scale_body, shape(1, feats, dtype=F32), (routed1, routed2, damping), 4 * slab * feats
        )
    with jax.named_scope("update"):
        operands = (part1, part2, other1, other2, routed1, routed2, scale, kept, keep)
        out = pl.pallas_call(
            functools.partial(update_body, 2),
            out_shape=shape(slab, feats),
            in_specs=[vmem] * len(operands),
            out_specs=hbm,
            scratch_shapes=[
                pltpu.VMEM((slab, feats), BF16),
                pltpu.SemaphoreType.DMA((feats // WIDTH,)),
            ],
            compiler_params=pltpu.CompilerParams(vmem_limit_bytes=VMEM),
        )(*operands)
    return out.reshape(1, slab, feats)


def solution(mesh):
    n_hrow, n_hcol = mesh.shape["hrow"], mesh.shape["hcol"]
    n_expert = mesh.shape["expert"]
    fine = Mesh(
        mesh.devices.reshape(n_expert // 2, 2, n_hrow // 2, 2, n_hcol),
        ("z", "yh", "x", "core", "yl"),
    )
    own = ("z", "yh", "x", "core")
    in_specs = (P(own, "yl"), P(own, None), P(own, None, "yl"), P(None, "yl"), P(own, "yl"))
    return jax.shard_map(
        local, mesh=fine, in_specs=in_specs, out_specs=P(own, None, "yl"), check_vma=False
    )
```

```python
import functools

import jax
import jax.numpy as jnp
from jax import lax
from jax.experimental import pallas as pl
from jax.experimental.pallas import tpu as pltpu
from jax.sharding import Mesh, PartitionSpec as P

ROWS_E = 128
ETA = 0.5
CAP = 2
LANES = 128
WIDTH = 896
VMEM = 16 * 2**20
F32 = jnp.float32
BF16 = jnp.bfloat16


def call(body, out_shape, operands, flops, scratch=(), name=None):
    size = sum(o.size * o.dtype.itemsize for o in operands)
    outs = jax.tree.leaves(out_shape)
    size += sum(o.size * o.dtype.itemsize for o in outs)
    return pl.pallas_call(
        body,
        out_shape=out_shape,
        in_specs=[pl.BlockSpec(memory_space=pltpu.VMEM)] * len(operands),
        out_specs=jax.tree.map(lambda _: pl.BlockSpec(memory_space=pltpu.VMEM), out_shape),
        scratch_shapes=list(scratch),
        cost_estimate=pl.CostEstimate(flops=flops, bytes_accessed=size, transcendentals=0),
        compiler_params=pltpu.CompilerParams(vmem_limit_bytes=VMEM),
        name=name,
    )(*operands)


def tag_body(tokens_hbm, ids_hbm, out_ref, ids_ref, sems):
    feats = tokens_hbm.shape[1]
    top = ids_ref.shape[0]
    get_ids = pltpu.make_async_copy(ids_hbm, ids_ref, sems.at[0])
    get_tokens = pltpu.make_async_copy(tokens_hbm, out_ref.at[:, pl.ds(0, feats)], sems.at[1])
    get_ids.start()
    get_tokens.start()
    spread = (
        lax.broadcasted_iota(jnp.int32, (top, LANES), 0)
        == lax.broadcasted_iota(jnp.int32, (top, LANES), 1)
    ).astype(BF16)
    get_ids.wait()
    ids = ids_ref[...].astype(F32).astype(BF16)
    out_ref[:, feats:] = lax.dot_general(
        ids, spread, (((0,), (0,)), ((), ())), preferred_element_type=F32
    ).astype(BF16)
    get_tokens.wait()


def pack_body(tok_rows, top, first_ref, held, out_hbm, out_ref, sems):
    rows, feats = out_ref.shape
    tokens = held.shape[0]
    per_dest = tokens // tok_rows * CAP
    pick = (
        lax.broadcasted_iota(jnp.int32, (top, LANES), 0)
        == lax.broadcasted_iota(jnp.int32, (top, LANES), 1)
    ).astype(BF16)
    ids = lax.dot_general(
        pick, held[:, feats:], (((1,), (1,)), ((), ())), preferred_element_type=F32
    )
    row = lax.broadcasted_iota(jnp.int32, (rows, 1), 0)
    expert = (first_ref[0] + row // per_dest).astype(F32)
    block = (row % per_dest) // CAP
    slot = (row % CAP).astype(F32)
    tok = lax.broadcasted_iota(jnp.int32, (1, tokens), 1)
    named = ids[0:1, :] == expert
    for k in range(1, top):
        named = named | (ids[k : k + 1, :] == expert)
    named = named & (tok // tok_rows == block)
    member = jnp.where(named, 1.0, 0.0)
    before = (
        lax.broadcasted_iota(jnp.int32, (tokens, tokens), 0)
        < lax.broadcasted_iota(jnp.int32, (tokens, tokens), 1)
    ).astype(BF16)
    rank = jnp.dot(member.astype(BF16), before, preferred_element_type=F32)
    select = jnp.where(rank == slot, member, 0.0).astype(BF16)
    copies = []
    for i, lo in enumerate(range(0, feats, WIDTH)):
        cols = (slice(None), pl.ds(lo, WIDTH))
        out_ref[cols] = jnp.dot(select, held[cols], preferred_element_type=F32).astype(BF16)
        copies.append(pltpu.make_async_copy(out_ref.at[cols], out_hbm.at[cols], sems.at[i]))
        copies[-1].start()
    for copy in copies:
        copy.wait()


def prune_body(weight_ref, bits_ref, *refs):
    *pruned_refs, kept_ref, keep_ref = refs
    rows, words = bits_ref.shape
    feats = weight_ref.shape[1]
    lane = lax.broadcasted_iota(jnp.int32, (rows, LANES), 1)
    bits = jnp.concatenate([bits_ref[...], jnp.zeros((rows, LANES - words), jnp.int32)], axis=1)
    for j in range(feats // LANES):
        word = jnp.take_along_axis(bits, lane // 32 + 4 * j, axis=1, mode="promise_in_bounds")
        keep = jnp.bitwise_and(jnp.right_shift(word, lane % 32), 1).astype(F32)
        cols = slice(j * LANES, (j + 1) * LANES)
        slab = weight_ref[:, cols].astype(F32)
        piece, at = divmod(j * LANES, WIDTH)
        pruned_refs[piece][:, at : at + LANES] = jnp.where(keep > 0.5, 0.0, slab).astype(BF16)
        kept_ref[:, cols] = jnp.where(keep > 0.5, slab, 0.0).astype(BF16)
        keep_ref[:, cols] = keep.astype(BF16)


def project_body(routed_ref, *refs):
    *pruned_refs, part_ref, low_ref = refs
    part = None
    for i, ref in enumerate(pruned_refs):
        term = lax.dot_general(
            ref[...],
            routed_ref[:, i * WIDTH : (i + 1) * WIDTH],
            (((1,), (1,)), ((), ())),
            preferred_element_type=F32,
        )
        part = term if part is None else part + term
    part_ref[...] = part
    low_ref[...] = part.astype(BF16)


def scale_body(*refs):
    *routed_refs, damping_ref, scale_ref = refs
    feats = damping_ref.shape[1]
    for lo in range(0, feats, WIDTH):
        cols = slice(lo, lo + WIDTH)
        diag = damping_ref[:, cols]
        for ref in routed_refs:
            rows = ref[:, cols].astype(F32)
            diag = diag + jnp.sum(rows * rows, axis=0, keepdims=True) * (1.0 / ROWS_E)
        scale_ref[:, cols] = (ETA / ROWS_E) / diag


def update_body(n, *refs):
    parts, others, routed_refs = refs[:n], refs[n : 2 * n], refs[2 * n : 3 * n]
    scale_ref, kept_ref, keep_ref, out_hbm, out_ref, sems = refs[3 * n :]
    feats = kept_ref.shape[1]
    projected = [(p[...] + o[...].astype(F32)).astype(BF16) for p, o in zip(parts, others)]
    copies = []
    for i, lo in enumerate(range(0, feats, WIDTH)):
        cols = slice(lo, lo + WIDTH)
        comp = jnp.dot(projected[0], routed_refs[0][:, cols], preferred_element_type=F32)
        for p, r in zip(projected[1:], routed_refs[1:]):
            comp = comp + jnp.dot(p, r[:, cols], preferred_element_type=F32)
        gain = keep_ref[:, cols].astype(F32) * (comp * scale_ref[:, cols])
        out_ref[:, cols] = (kept_ref[:, cols].astype(F32) + gain).astype(BF16)
        cols = (slice(None), pl.ds(lo, WIDTH))
        copies.append(pltpu.make_async_copy(out_ref.at[cols], out_hbm.at[cols], sems.at[i]))
        copies[-1].start()
    for copy in copies:
        copy.wait()


def shape(*dims, dtype=BF16):
    return jax.ShapeDtypeStruct(dims, dtype)


def shift(x, axis, step):
    n = lax.axis_size(axis)
    return lax.ppermute(x, axis, [(i, (i + step) % n) for i in range(n)])


def local(tokens, expert_ids, weight, mask_bits, damping):
    tok_rows, feats = tokens.shape
    top = expert_ids.shape[1]
    slab = weight.shape[1]
    weight = weight.reshape(slab, feats)
    near = ("zl", "yh", "x", "core")
    dests = lax.axis_size(near)
    n_tok = tok_rows * lax.axis_size("zh")
    rows = dests * lax.axis_size("zh") * CAP
    pieces = feats // WIDTH
    first = (lax.axis_index("zh") * dests).astype(jnp.int32).reshape(1)
    hbm, vmem = pl.BlockSpec(memory_space=pltpu.HBM), pl.BlockSpec(memory_space=pltpu.VMEM)
    params = pltpu.CompilerParams(vmem_limit_bytes=VMEM)

    with jax.named_scope("tag"):
        own = pl.pallas_call(
            tag_body,
            out_shape=shape(tok_rows, feats + LANES),
            in_specs=[hbm, hbm],
            out_specs=vmem,
            scratch_shapes=[
                pltpu.VMEM((top, tok_rows), jnp.int32),
                pltpu.SemaphoreType.DMA((2,)),
            ],
            compiler_params=params,
        )(tokens, expert_ids.T)
    with jax.named_scope("gather"):
        held = lax.all_gather(own, "zh", tiled=True)
    with jax.named_scope("pack"):
        packed = pl.pallas_call(
            functools.partial(pack_body, tok_rows, top),
            out_shape=pltpu.HBM((rows, feats), BF16),
            in_specs=[pl.BlockSpec(memory_space=pltpu.SMEM), vmem],
            out_specs=hbm,
            scratch_shapes=[pltpu.VMEM((rows, feats), BF16), pltpu.SemaphoreType.DMA((pieces,))],
            compiler_params=params,
        )(first, held)
    with jax.named_scope("route"):
        block = lax.all_to_all(
            packed.reshape(dests, -1, feats), near, split_axis=0, concat_axis=0, tiled=True
        )
    routed = block.reshape(rows, feats)
    with jax.named_scope("prune"):
        *pruned, kept, keep = call(
            prune_body,
            (shape(slab, WIDTH),) * pieces + (shape(slab, feats),) * 2,
            (weight, mask_bits),
            1 << 22,
        )
    with jax.named_scope("project"):
        part, low = call(
            project_body,
            (shape(slab, rows, dtype=F32), shape(slab, rows)),
            (routed, *pruned),
            2 * rows * slab * feats,
        )
    with jax.named_scope("swap_features"):
        other = shift(low, "yl", 1)
    with jax.named_scope("scale"):
        scale = call(
            scale_body, shape(1, feats, dtype=F32), (routed, damping), 4 * slab * feats
        )
    with jax.named_scope("update"):
        operands = (part, other, routed, scale, kept, keep)
        out = pl.pallas_call(
            functools.partial(update_body, 1),
            out_shape=shape(slab, feats),
            in_specs=[vmem] * len(operands),
            out_specs=hbm,
            scratch_shapes=[pltpu.VMEM((slab, feats), BF16), pltpu.SemaphoreType.DMA((pieces,))],
            compiler_params=params,
        )(*operands)
    return out.reshape(1, slab, feats)


def solution(mesh):
    n_hrow, n_hcol = mesh.shape["hrow"], mesh.shape["hcol"]
    n_expert = mesh.shape["expert"]
    fine = Mesh(
        mesh.devices.reshape(n_expert // 4, 2, 2, n_hrow // 2, 2, n_hcol),
        ("zh", "zl", "yh", "x", "core", "yl"),
    )
    own = ("zh", "zl", "yh", "x", "core")
    in_specs = (P(own, "yl"), P(own, None), P(own, None, "yl"), P(None, "yl"), P(own, "yl"))
    return jax.shard_map(
        local, mesh=fine, in_specs=in_specs, out_specs=P(own, None, "yl"), check_vma=False
    )
```

```python
import functools

import jax
import jax.numpy as jnp
from jax import lax
from jax.experimental import pallas as pl
from jax.experimental.pallas import tpu as pltpu
from jax.sharding import Mesh, PartitionSpec as P

ROWS_E = 128
ETA = 0.5
CAP = 2
LANES = 128
WIDTH = 896
STEP = 512
VMEM = 16 * 2**20
F32 = jnp.float32
BF16 = jnp.bfloat16


def call(body, out_shape, operands, flops, scratch=(), name=None):
    size = sum(o.size * o.dtype.itemsize for o in operands)
    outs = jax.tree.leaves(out_shape)
    size += sum(o.size * o.dtype.itemsize for o in outs)
    return pl.pallas_call(
        body,
        out_shape=out_shape,
        in_specs=[pl.BlockSpec(memory_space=pltpu.VMEM)] * len(operands),
        out_specs=jax.tree.map(lambda _: pl.BlockSpec(memory_space=pltpu.VMEM), out_shape),
        scratch_shapes=list(scratch),
        cost_estimate=pl.CostEstimate(flops=flops, bytes_accessed=size, transcendentals=0),
        compiler_params=pltpu.CompilerParams(vmem_limit_bytes=VMEM),
        name=name,
    )(*operands)


def tag_body(tokens_hbm, ids_hbm, out_ref, ids_ref, sems):
    feats = tokens_hbm.shape[1]
    top = ids_ref.shape[0]
    get_ids = pltpu.make_async_copy(ids_hbm, ids_ref, sems.at[0])
    get_tokens = pltpu.make_async_copy(tokens_hbm, out_ref.at[:, pl.ds(0, feats)], sems.at[1])
    get_ids.start()
    get_tokens.start()
    spread = (
        lax.broadcasted_iota(jnp.int32, (top, LANES), 0)
        == lax.broadcasted_iota(jnp.int32, (top, LANES), 1)
    ).astype(BF16)
    get_ids.wait()
    ids = ids_ref[...].astype(F32).astype(BF16)
    out_ref[:, feats:] = lax.dot_general(
        ids, spread, (((0,), (0,)), ((), ())), preferred_element_type=F32
    ).astype(BF16)
    get_tokens.wait()


def pack_body(tok_rows, top, first_ref, held, out_hbm, out_ref, sems):
    rows, feats = out_ref.shape
    tokens = held.shape[0]
    per_dest = tokens // tok_rows * CAP
    pick = (
        lax.broadcasted_iota(jnp.int32, (top, LANES), 0)
        == lax.broadcasted_iota(jnp.int32, (top, LANES), 1)
    ).astype(BF16)
    ids = lax.dot_general(
        pick, held[:, feats:], (((1,), (1,)), ((), ())), preferred_element_type=F32
    )
    row = lax.broadcasted_iota(jnp.int32, (rows, 1), 0)
    expert = (first_ref[0] + row // per_dest).astype(F32)
    block = (row % per_dest) // CAP
    slot = (row % CAP).astype(F32)
    tok = lax.broadcasted_iota(jnp.int32, (1, tokens), 1)
    named = ids[0:1, :] == expert
    for k in range(1, top):
        named = named | (ids[k : k + 1, :] == expert)
    named = named & (tok // tok_rows == block)
    member = jnp.where(named, 1.0, 0.0)
    before = (
        lax.broadcasted_iota(jnp.int32, (tokens, tokens), 0)
        < lax.broadcasted_iota(jnp.int32, (tokens, tokens), 1)
    ).astype(BF16)
    rank = jnp.dot(member.astype(BF16), before, preferred_element_type=F32)
    select = jnp.where(rank == slot, member, 0.0).astype(BF16)
    copies = []
    for i, lo in enumerate(range(0, feats, STEP)):
        cols = (slice(None), pl.ds(lo, STEP))
        out_ref[cols] = jnp.dot(select, held[cols], preferred_element_type=F32).astype(BF16)
        copies.append(pltpu.make_async_copy(out_ref.at[cols], out_hbm.at[cols], sems.at[i]))
        copies[-1].start()
    for copy in copies:
        copy.wait()


def prune_body(weight_ref, bits_ref, *refs):
    *pruned_refs, kept_ref, keep_ref = refs
    rows, words = bits_ref.shape
    feats = weight_ref.shape[1]
    lane = lax.broadcasted_iota(jnp.int32, (rows, LANES), 1)
    bits = jnp.concatenate([bits_ref[...], jnp.zeros((rows, LANES - words), jnp.int32)], axis=1)
    for j in range(feats // LANES):
        word = jnp.take_along_axis(bits, lane // 32 + 4 * j, axis=1, mode="promise_in_bounds")
        keep = jnp.bitwise_and(jnp.right_shift(word, lane % 32), 1).astype(F32)
        cols = slice(j * LANES, (j + 1) * LANES)
        slab = weight_ref[:, cols].astype(F32)
        piece, at = divmod(j * LANES, WIDTH)
        pruned_refs[piece][:, at : at + LANES] = jnp.where(keep > 0.5, 0.0, slab).astype(BF16)
        kept_ref[:, cols] = jnp.where(keep > 0.5, slab, 0.0).astype(BF16)
        keep_ref[:, cols] = keep.astype(BF16)


def project_body(routed_ref, *refs):
    *pruned_refs, last_hbm, part_ref, low_ref, last_ref, sem = refs
    fetch = pltpu.make_async_copy(last_hbm, last_ref, sem)
    fetch.start()
    part = jnp.zeros(part_ref.shape, F32)
    for i, ref in enumerate((*pruned_refs, last_ref)):
        if ref is last_ref:
            fetch.wait()
        part = part + lax.dot_general(
            ref[...],
            routed_ref[:, i * WIDTH : (i + 1) * WIDTH],
            (((1,), (1,)), ((), ())),
            preferred_element_type=F32,
        )
    part_ref[...] = part
    low_ref[...] = part.astype(BF16)


def scale_body(*refs):
    *routed_refs, damping_ref, scale_ref = refs
    feats = damping_ref.shape[1]
    for lo in range(0, feats, WIDTH):
        cols = slice(lo, lo + WIDTH)
        diag = damping_ref[:, cols]
        for ref in routed_refs:
            rows = ref[:, cols].astype(F32)
            diag = diag + jnp.sum(rows * rows, axis=0, keepdims=True) * (1.0 / ROWS_E)
        scale_ref[:, cols] = (ETA / ROWS_E) / diag


def update_body(n, *refs):
    parts, others, routed_refs = refs[:n], refs[n : 2 * n], refs[2 * n : 3 * n]
    scale_ref, kept_ref, keep_ref, out_hbm, out_ref, sems = refs[3 * n :]
    feats = kept_ref.shape[1]
    projected = [(p[...] + o[...].astype(F32)).astype(BF16) for p, o in zip(parts, others)]
    copies = []
    for i, lo in enumerate(range(0, feats, STEP)):
        cols = slice(lo, lo + STEP)
        comp = jnp.dot(projected[0], routed_refs[0][:, cols], preferred_element_type=F32)
        for p, r in zip(projected[1:], routed_refs[1:]):
            comp = comp + jnp.dot(p, r[:, cols], preferred_element_type=F32)
        gain = keep_ref[:, cols].astype(F32) * (comp * scale_ref[:, cols])
        out_ref[:, cols] = (kept_ref[:, cols].astype(F32) + gain).astype(BF16)
        cols = (slice(None), pl.ds(lo, STEP))
        copies.append(pltpu.make_async_copy(out_ref.at[cols], out_hbm.at[cols], sems.at[i]))
        copies[-1].start()
    for copy in copies:
        copy.wait()


def shape(*dims, dtype=BF16):
    return jax.ShapeDtypeStruct(dims, dtype)


def in_hbm(x):
    return pltpu.with_memory_space_constraint(x, pltpu.HBM)


def shift(x, axis, step):
    n = lax.axis_size(axis)
    return lax.ppermute(x, axis, [(i, (i + step) % n) for i in range(n)])


def local(tokens, expert_ids, weight, mask_bits, damping):
    tok_rows, feats = tokens.shape
    top = expert_ids.shape[1]
    slab = weight.shape[1]
    weight = weight.reshape(slab, feats)
    near = ("zl", "yh", "x", "core")
    dests = lax.axis_size(near)
    n_tok = tok_rows * lax.axis_size("zh")
    rows = dests * lax.axis_size("zh") * CAP
    pieces = feats // WIDTH
    first = (lax.axis_index("zh") * dests).astype(jnp.int32).reshape(1)
    hbm, vmem = pl.BlockSpec(memory_space=pltpu.HBM), pl.BlockSpec(memory_space=pltpu.VMEM)
    params = pltpu.CompilerParams(vmem_limit_bytes=VMEM)

    with jax.named_scope("tag"):
        own = pl.pallas_call(
            tag_body,
            out_shape=shape(tok_rows, feats + LANES),
            in_specs=[hbm, hbm],
            out_specs=vmem,
            scratch_shapes=[
                pltpu.VMEM((top, tok_rows), jnp.int32),
                pltpu.SemaphoreType.DMA((2,)),
            ],
            compiler_params=params,
        )(in_hbm(tokens), in_hbm(expert_ids.T))
    with jax.named_scope("gather"):
        held = lax.all_gather(own, "zh", tiled=True)
    with jax.named_scope("pack"):
        packed = pl.pallas_call(
            functools.partial(pack_body, tok_rows, top),
            out_shape=pltpu.HBM((rows, feats), BF16),
            in_specs=[pl.BlockSpec(memory_space=pltpu.SMEM), vmem],
            out_specs=hbm,
            scratch_shapes=[
                pltpu.VMEM((rows, feats), BF16),
                pltpu.SemaphoreType.DMA((feats // STEP,)),
            ],
            compiler_params=params,
        )(first, held)
    with jax.named_scope("route"):
        block = lax.all_to_all(
            packed.reshape(dests, -1, feats), near, split_axis=0, concat_axis=0, tiled=True
        )
    routed = block.reshape(rows, feats)
    with jax.named_scope("prune"):
        *pruned, kept, keep = call(
            prune_body,
            (shape(slab, WIDTH),) * pieces + (shape(slab, feats),) * 2,
            (weight, mask_bits),
            1 << 22,
        )
    with jax.named_scope("project"):
        part, low = pl.pallas_call(
            project_body,
            out_shape=(shape(slab, rows, dtype=F32), shape(slab, rows)),
            in_specs=[vmem] * pieces + [hbm],
            out_specs=(vmem, vmem),
            scratch_shapes=[pltpu.VMEM((slab, WIDTH), BF16), pltpu.SemaphoreType.DMA],
            cost_estimate=pl.CostEstimate(
                flops=2 * rows * slab * feats, bytes_accessed=1 << 22, transcendentals=0
            ),
            compiler_params=params,
        )(routed, *pruned[:-1], in_hbm(pruned[-1]))
    with jax.named_scope("swap_features"):
        other = shift(low, "yl", 1)
    with jax.named_scope("scale"):
        scale = call(
            scale_body, shape(1, feats, dtype=F32), (routed, damping), 4 * slab * feats
        )
    with jax.named_scope("update"):
        operands = (part, other, routed, scale, kept, keep)
        out = pl.pallas_call(
            functools.partial(update_body, 1),
            out_shape=shape(slab, feats),
            in_specs=[vmem] * len(operands),
            out_specs=hbm,
            scratch_shapes=[
                pltpu.VMEM((slab, feats), BF16),
                pltpu.SemaphoreType.DMA((feats // STEP,)),
            ],
            compiler_params=params,
        )(*operands)
    return out.reshape(1, slab, feats)


def solution(mesh):
    n_hrow, n_hcol = mesh.shape["hrow"], mesh.shape["hcol"]
    n_expert = mesh.shape["expert"]
    fine = Mesh(
        mesh.devices.reshape(n_expert // 4, 2, 2, n_hrow // 2, 2, n_hcol),
        ("zh", "zl", "yh", "x", "core", "yl"),
    )
    own = ("zh", "zl", "yh", "x", "core")
    in_specs = (P(own, "yl"), P(own, None), P(own, None, "yl"), P(None, "yl"), P(own, "yl"))
    return jax.shard_map(
        local, mesh=fine, in_specs=in_specs, out_specs=P(own, None, "yl"), check_vma=False
    )
```

```python
import functools

import jax
import jax.numpy as jnp
from jax import lax
from jax.experimental import pallas as pl
from jax.experimental.pallas import tpu as pltpu
from jax.sharding import Mesh, PartitionSpec as P

ROWS_E = 128
ETA = 0.5
CAP = 2
LANES = 128
STEP = 512
PARTS = 2
VMEM = 16 * 2**20
F32 = jnp.float32
BF16 = jnp.bfloat16


def call(body, out_shape, operands, flops, scratch=(), name=None):
    size = sum(o.size * o.dtype.itemsize for o in operands)
    outs = jax.tree.leaves(out_shape)
    size += sum(o.size * o.dtype.itemsize for o in outs)
    return pl.pallas_call(
        body,
        out_shape=out_shape,
        in_specs=[pl.BlockSpec(memory_space=pltpu.VMEM)] * len(operands),
        out_specs=jax.tree.map(lambda _: pl.BlockSpec(memory_space=pltpu.VMEM), out_shape),
        scratch_shapes=list(scratch),
        cost_estimate=pl.CostEstimate(flops=flops, bytes_accessed=size, transcendentals=0),
        compiler_params=pltpu.CompilerParams(vmem_limit_bytes=VMEM),
        name=name,
    )(*operands)


def tag_body(tokens_hbm, ids_hbm, out_ref, ids_ref, sems):
    feats = tokens_hbm.shape[1]
    top = ids_ref.shape[0]
    get_ids = pltpu.make_async_copy(ids_hbm, ids_ref, sems.at[0])
    get_tokens = pltpu.make_async_copy(tokens_hbm, out_ref.at[:, pl.ds(0, feats)], sems.at[1])
    get_ids.start()
    get_tokens.start()
    spread = (
        lax.broadcasted_iota(jnp.int32, (top, LANES), 0)
        == lax.broadcasted_iota(jnp.int32, (top, LANES), 1)
    ).astype(BF16)
    get_ids.wait()
    ids = ids_ref[...].astype(F32).astype(BF16)
    out_ref[:, feats:] = lax.dot_general(
        ids, spread, (((0,), (0,)), ((), ())), preferred_element_type=F32
    ).astype(BF16)
    get_tokens.wait()


def pack_body(tok_rows, top, first_ref, held, out_hbm, out_ref, sems):
    rows, feats = out_ref.shape
    tokens = held.shape[0]
    per_dest = tokens // tok_rows * CAP
    pick = (
        lax.broadcasted_iota(jnp.int32, (top, LANES), 0)
        == lax.broadcasted_iota(jnp.int32, (top, LANES), 1)
    ).astype(BF16)
    ids = lax.dot_general(
        pick, held[:, feats:], (((1,), (1,)), ((), ())), preferred_element_type=F32
    )
    row = lax.broadcasted_iota(jnp.int32, (rows, 1), 0)
    expert = (first_ref[0] + row // per_dest).astype(F32)
    block = (row % per_dest) // CAP
    slot = (row % CAP).astype(F32)
    tok = lax.broadcasted_iota(jnp.int32, (1, tokens), 1)
    named = ids[0:1, :] == expert
    for k in range(1, top):
        named = named | (ids[k : k + 1, :] == expert)
    named = named & (tok // tok_rows == block)
    member = jnp.where(named, 1.0, 0.0)
    before = (
        lax.broadcasted_iota(jnp.int32, (tokens, tokens), 0)
        < lax.broadcasted_iota(jnp.int32, (tokens, tokens), 1)
    ).astype(BF16)
    rank = jnp.dot(member.astype(BF16), before, preferred_element_type=F32)
    select = jnp.where(rank == slot, member, 0.0).astype(BF16)
    copies = []
    for i, lo in enumerate(range(0, feats, STEP)):
        cols = (slice(None), pl.ds(lo, STEP))
        out_ref[cols] = jnp.dot(select, held[cols], preferred_element_type=F32).astype(BF16)
        copies.append(pltpu.make_async_copy(out_ref.at[cols], out_hbm.at[cols], sems.at[i]))
        copies[-1].start()
    for copy in copies:
        copy.wait()


def prune_body(weight_ref, bits_ref, *refs):
    *pruned_refs, rest_ref, kept_ref = refs
    rows, words = bits_ref.shape
    part = rows // len(pruned_refs)
    wide = pruned_refs[-1].shape[1]
    lane = lax.broadcasted_iota(jnp.int32, (rows, LANES), 1)
    bits = jnp.concatenate([bits_ref[...], jnp.zeros((rows, LANES - words), jnp.int32)], axis=1)
    for j in range(weight_ref.shape[1] // LANES):
        word = jnp.take_along_axis(bits, lane // 32 + 4 * j, axis=1, mode="promise_in_bounds")
        keep = jnp.bitwise_and(jnp.right_shift(word, lane % 32), 1) == 1
        lo = j * LANES
        cols = slice(lo, lo + LANES)
        slab = weight_ref[:, cols].astype(F32)
        pruned = jnp.where(keep, 0.0, slab).astype(BF16)
        for i, ref in enumerate(pruned_refs):
            mine = pruned[i * part : (i + 1) * part]
            if lo < ref.shape[1]:
                ref[:, cols] = mine
            else:
                rest_ref[:, lo - wide : lo - wide + LANES] = mine
        kept_ref[:, cols] = jnp.where(keep, slab, jnp.inf).astype(BF16)


def project_body(routed_ref, pruned_ref, *refs):
    *rest, part_ref, low_ref = refs[:3] if len(refs) > 2 else refs
    wide = pruned_ref.shape[1]
    if rest:
        rest_ref, sem = refs[3:]
        fetch = pltpu.make_async_copy(rest[0], rest_ref, sem)
        fetch.start()
    part = lax.dot_general(
        pruned_ref[...],
        routed_ref[:, :wide],
        (((1,), (1,)), ((), ())),
        preferred_element_type=F32,
    )
    if rest:
        fetch.wait()
        part = part + lax.dot_general(
            rest_ref[...],
            routed_ref[:, wide:],
            (((1,), (1,)), ((), ())),
            preferred_element_type=F32,
        )
    part_ref[...] = part
    low_ref[...] = part.astype(BF16)


def scale_body(*refs):
    *routed_refs, damping_ref, scale_ref = refs
    feats = damping_ref.shape[1]
    for lo in range(0, feats, STEP):
        cols = slice(lo, lo + STEP)
        diag = damping_ref[:, cols]
        for ref in routed_refs:
            rows = ref[:, cols].astype(F32)
            diag = diag + jnp.sum(rows * rows, axis=0, keepdims=True) * (1.0 / ROWS_E)
        scale_ref[:, cols] = (ETA / ROWS_E) / diag


def update_body(at, part_ref, other_ref, routed_ref, scale_ref, kept_ref, *refs):
    out_hbm, out_ref, sems = refs[-3:]
    rows, feats = out_ref.shape
    mine = slice(at, at + rows)
    projected = (part_ref[...] + other_ref[...].astype(F32)).astype(BF16)
    copies = []
    for i, lo in enumerate(range(0, feats, STEP)):
        cols = slice(lo, lo + STEP)
        comp = jnp.dot(projected, routed_ref[:, cols], preferred_element_type=F32)
        kept = kept_ref[mine, cols].astype(F32)
        updated = jnp.where(kept < jnp.inf, kept + comp * scale_ref[:, cols], 0.0)
        out_ref[:, cols] = updated.astype(BF16)
        copies.append(
            pltpu.make_async_copy(
                out_ref.at[:, pl.ds(lo, STEP)],
                out_hbm.at[pl.ds(at, rows), pl.ds(lo, STEP)],
                sems.at[i],
            )
        )
        copies[-1].start()
    for copy in copies:
        copy.wait()


def shape(*dims, dtype=BF16):
    return jax.ShapeDtypeStruct(dims, dtype)


def in_hbm(x):
    return pltpu.with_memory_space_constraint(x, pltpu.HBM)


def shift(x, axis, step):
    n = lax.axis_size(axis)
    return lax.ppermute(x, axis, [(i, (i + step) % n) for i in range(n)])


def local(tokens, expert_ids, weight, mask_bits, damping):
    tok_rows, feats = tokens.shape
    top = expert_ids.shape[1]
    slab = weight.shape[1]
    weight = weight.reshape(slab, feats)
    near = ("zl", "yh", "x", "core")
    dests = lax.axis_size(near)
    n_tok = tok_rows * lax.axis_size("zh")
    rows = dests * lax.axis_size("zh") * CAP
    first = (lax.axis_index("zh") * dests).astype(jnp.int32).reshape(1)
    hbm, vmem = pl.BlockSpec(memory_space=pltpu.HBM), pl.BlockSpec(memory_space=pltpu.VMEM)
    params = pltpu.CompilerParams(vmem_limit_bytes=VMEM)

    with jax.named_scope("tag"):
        own = pl.pallas_call(
            tag_body,
            out_shape=shape(tok_rows, feats + LANES),
            in_specs=[hbm, hbm],
            out_specs=vmem,
            scratch_shapes=[
                pltpu.VMEM((top, tok_rows), jnp.int32),
                pltpu.SemaphoreType.DMA((2,)),
            ],
            compiler_params=params,
        )(in_hbm(tokens), in_hbm(expert_ids.T))
    with jax.named_scope("gather"):
        held = lax.all_gather(own, "zh", tiled=True)
    with jax.named_scope("pack"):
        packed = pl.pallas_call(
            functools.partial(pack_body, tok_rows, top),
            out_shape=pltpu.HBM((rows, feats), BF16),
            in_specs=[pl.BlockSpec(memory_space=pltpu.SMEM), vmem],
            out_specs=hbm,
            scratch_shapes=[
                pltpu.VMEM((rows, feats), BF16),
                pltpu.SemaphoreType.DMA((feats // STEP,)),
            ],
            compiler_params=params,
        )(first, held)
    with jax.named_scope("route"):
        block = lax.all_to_all(
            packed.reshape(dests, -1, feats), near, split_axis=0, concat_axis=0, tiled=True
        )
    routed = block.reshape(rows, feats)
    part_rows = slab // PARTS
    with jax.named_scope("prune"):
        *pruned, rest, kept = call(
            prune_body,
            (shape(part_rows, feats),) * (PARTS - 1)
            + (shape(part_rows, feats - STEP), shape(part_rows, STEP), shape(slab, feats)),
            (weight, mask_bits),
            1 << 22,
        )
    parts = []
    for i, p in enumerate(pruned):
        last = i == PARTS - 1
        if i:
            p = lax.optimization_barrier((p, parts[-1][1]))[0]
        with jax.named_scope("project"):
            parts.append(
                pl.pallas_call(
                    project_body,
                    out_shape=(shape(part_rows, rows, dtype=F32), shape(part_rows, rows)),
                    in_specs=[vmem, vmem] + [hbm] * last,
                    out_specs=(vmem, vmem),
                    scratch_shapes=[pltpu.VMEM(rest.shape, BF16), pltpu.SemaphoreType.DMA] * last,
                    cost_estimate=pl.CostEstimate(
                        flops=2 * rows * part_rows * feats,
                        bytes_accessed=1 << 21,
                        transcendentals=0,
                    ),
                    compiler_params=params,
                )(routed, p, *([in_hbm(rest)] if last else []))
            )
    with jax.named_scope("swap_features"):
        others = [shift(low, "yl", 1) for _, low in parts]
    with jax.named_scope("scale"):
        scale = call(
            scale_body, shape(1, feats, dtype=F32), (routed, damping), 4 * slab * feats
        )
    out = None
    for i, ((part, _), other) in enumerate(zip(parts, others)):
        operands = (part, other, routed, scale, kept)
        with jax.named_scope("update"):
            out = pl.pallas_call(
                functools.partial(update_body, i * part_rows),
                out_shape=pltpu.HBM((slab, feats), BF16),
                in_specs=[vmem] * len(operands) + [hbm] * (i > 0),
                out_specs=hbm,
                scratch_shapes=[
                    pltpu.VMEM((part_rows, feats), BF16),
                    pltpu.SemaphoreType.DMA((feats // STEP,)),
                ],
                input_output_aliases={len(operands): 0} if i else {},
                cost_estimate=pl.CostEstimate(
                    flops=2 * rows * part_rows * feats,
                    bytes_accessed=1 << 22,
                    transcendentals=0,
                ),
                compiler_params=params,
            )(*operands, *([in_hbm(out)] if i else []))
    return out.reshape(1, slab, feats)


def solution(mesh):
    n_hrow, n_hcol = mesh.shape["hrow"], mesh.shape["hcol"]
    n_expert = mesh.shape["expert"]
    fine = Mesh(
        mesh.devices.reshape(n_expert // 4, 2, 2, n_hrow // 2, 2, n_hcol),
        ("zh", "zl", "yh", "x", "core", "yl"),
    )
    own = ("zh", "zl", "yh", "x", "core")
    in_specs = (P(own, "yl"), P(own, None), P(own, None, "yl"), P(None, "yl"), P(own, "yl"))
    return jax.shard_map(
        local, mesh=fine, in_specs=in_specs, out_specs=P(own, None, "yl"), check_vma=False
    )
```

```python
import functools

import jax
import jax.numpy as jnp
from jax import lax
from jax.experimental import pallas as pl
from jax.experimental.pallas import tpu as pltpu
from jax.sharding import Mesh, PartitionSpec as P

ROWS_E = 128
ETA = 0.5
CAP = 2
LANES = 128
STEP = 512
PARTS = 2
VMEM = 16 * 2**20
F32 = jnp.float32
BF16 = jnp.bfloat16


def call(body, out_shape, operands, flops, scratch=(), name=None):
    size = sum(o.size * o.dtype.itemsize for o in operands)
    outs = jax.tree.leaves(out_shape)
    size += sum(o.size * o.dtype.itemsize for o in outs)
    return pl.pallas_call(
        body,
        out_shape=out_shape,
        in_specs=[pl.BlockSpec(memory_space=pltpu.VMEM)] * len(operands),
        out_specs=jax.tree.map(lambda _: pl.BlockSpec(memory_space=pltpu.VMEM), out_shape),
        scratch_shapes=list(scratch),
        cost_estimate=pl.CostEstimate(flops=flops, bytes_accessed=size, transcendentals=0),
        compiler_params=pltpu.CompilerParams(vmem_limit_bytes=VMEM),
        name=name,
    )(*operands)


def tag_body(tokens_hbm, ids_hbm, out_ref, ids_ref, sems):
    feats = tokens_hbm.shape[1]
    top = ids_ref.shape[0]
    get_ids = pltpu.make_async_copy(ids_hbm, ids_ref, sems.at[0])
    get_tokens = pltpu.make_async_copy(tokens_hbm, out_ref.at[:, pl.ds(0, feats)], sems.at[1])
    get_ids.start()
    get_tokens.start()
    spread = (
        lax.broadcasted_iota(jnp.int32, (top, LANES), 0)
        == lax.broadcasted_iota(jnp.int32, (top, LANES), 1)
    ).astype(BF16)
    get_ids.wait()
    ids = ids_ref[...].astype(F32).astype(BF16)
    out_ref[:, feats:] = lax.dot_general(
        ids, spread, (((0,), (0,)), ((), ())), preferred_element_type=F32
    ).astype(BF16)
    get_tokens.wait()


def pack_body(tok_rows, top, first_ref, held, out_hbm, out_ref, sems):
    rows, feats = out_ref.shape
    tokens = held.shape[0]
    per_dest = tokens // tok_rows * CAP
    pick = (
        lax.broadcasted_iota(jnp.int32, (top, LANES), 0)
        == lax.broadcasted_iota(jnp.int32, (top, LANES), 1)
    ).astype(BF16)
    ids = lax.dot_general(
        pick, held[:, feats:], (((1,), (1,)), ((), ())), preferred_element_type=F32
    )
    row = lax.broadcasted_iota(jnp.int32, (rows, 1), 0)
    expert = (first_ref[0] + row // per_dest).astype(F32)
    block = (row % per_dest) // CAP
    slot = (row % CAP).astype(F32)
    tok = lax.broadcasted_iota(jnp.int32, (1, tokens), 1)
    named = ids[0:1, :] == expert
    for k in range(1, top):
        named = named | (ids[k : k + 1, :] == expert)
    named = named & (tok // tok_rows == block)
    member = jnp.where(named, 1.0, 0.0)
    before = (
        lax.broadcasted_iota(jnp.int32, (tokens, tokens), 0)
        < lax.broadcasted_iota(jnp.int32, (tokens, tokens), 1)
    ).astype(BF16)
    rank = jnp.dot(member.astype(BF16), before, preferred_element_type=F32)
    select = jnp.where(rank == slot, member, 0.0).astype(BF16)
    copies = []
    for i, lo in enumerate(range(0, feats, STEP)):
        cols = (slice(None), pl.ds(lo, STEP))
        out_ref[cols] = jnp.dot(select, held[cols], preferred_element_type=F32).astype(BF16)
        copies.append(pltpu.make_async_copy(out_ref.at[cols], out_hbm.at[cols], sems.at[i]))
        copies[-1].start()
    for copy in copies:
        copy.wait()


def prune_body(weight_ref, bits_ref, pruned_ref, rest_ref, kept_ref):
    rows, words = bits_ref.shape
    wide = pruned_ref.shape[1]
    lane = lax.broadcasted_iota(jnp.int32, (rows, LANES), 1)
    bits = jnp.concatenate([bits_ref[...], jnp.zeros((rows, LANES - words), jnp.int32)], axis=1)
    for j in range(weight_ref.shape[1] // LANES):
        word = jnp.take_along_axis(bits, lane // 32 + 4 * j, axis=1, mode="promise_in_bounds")
        keep = jnp.bitwise_and(jnp.right_shift(word, lane % 32), 1) == 1
        lo = j * LANES
        slab = weight_ref[:, lo : lo + LANES].astype(F32)
        pruned = jnp.where(keep, 0.0, slab).astype(BF16)
        if lo < wide:
            pruned_ref[:, lo : lo + LANES] = pruned
        else:
            rest_ref[:, lo - wide : lo - wide + LANES] = pruned
        kept_ref[:, lo : lo + LANES] = jnp.where(keep, slab, jnp.inf).astype(BF16)


def project_body(routed_ref, pruned_ref, rest_hbm, part_ref, *refs):
    *low_refs, rest_ref, sem = refs
    wide = pruned_ref.shape[1]
    fetch = pltpu.make_async_copy(rest_hbm, rest_ref, sem)
    fetch.start()
    dims = (((1,), (1,)), ((), ()))
    part = lax.dot_general(
        pruned_ref[...], routed_ref[:, :wide], dims, preferred_element_type=F32
    )
    fetch.wait()
    part = part + lax.dot_general(
        rest_ref[...], routed_ref[:, wide:], dims, preferred_element_type=F32
    )
    part_ref[...] = part
    rows = low_refs[0].shape[0]
    for i, ref in enumerate(low_refs):
        ref[...] = part[i * rows : (i + 1) * rows].astype(BF16)


def scale_body(routed_ref, damping_ref, kept_hbm, scale_ref, kept_ref, sem):
    fetch = pltpu.make_async_copy(kept_hbm, kept_ref, sem)
    fetch.start()
    feats = damping_ref.shape[1]
    for lo in range(0, feats, STEP):
        cols = slice(lo, lo + STEP)
        rows = routed_ref[:, cols].astype(F32)
        diag = jnp.sum(rows * rows, axis=0, keepdims=True) * (1.0 / ROWS_E) + damping_ref[:, cols]
        scale_ref[:, cols] = (ETA / ROWS_E) / diag
    fetch.wait()


def update_body(at, part_ref, other_ref, routed_ref, scale_ref, kept_ref, *refs):
    out_hbm, out_ref, sems = refs[-3:]
    rows, feats = out_ref.shape
    mine = slice(at, at + rows)
    projected = (part_ref[mine, :] + other_ref[...].astype(F32)).astype(BF16)
    copies = []
    for i, lo in enumerate(range(0, feats, STEP)):
        cols = slice(lo, lo + STEP)
        comp = jnp.dot(projected, routed_ref[:, cols], preferred_element_type=F32)
        kept = kept_ref[mine, cols].astype(F32)
        updated = jnp.where(kept < jnp.inf, kept + comp * scale_ref[:, cols], 0.0)
        out_ref[:, cols] = updated.astype(BF16)
        copies.append(
            pltpu.make_async_copy(
                out_ref.at[:, pl.ds(lo, STEP)],
                out_hbm.at[pl.ds(at, rows), pl.ds(lo, STEP)],
                sems.at[i],
            )
        )
        copies[-1].start()
    for copy in copies:
        copy.wait()


def shape(*dims, dtype=BF16):
    return jax.ShapeDtypeStruct(dims, dtype)


def in_hbm(x):
    return pltpu.with_memory_space_constraint(x, pltpu.HBM)


def shift(x, axis, step):
    n = lax.axis_size(axis)
    return lax.ppermute(x, axis, [(i, (i + step) % n) for i in range(n)])


def local(tokens, expert_ids, weight, mask_bits, damping):
    tok_rows, feats = tokens.shape
    top = expert_ids.shape[1]
    slab = weight.shape[1]
    weight = weight.reshape(slab, feats)
    near = ("zl", "yh", "x", "core")
    dests = lax.axis_size(near)
    n_tok = tok_rows * lax.axis_size("zh")
    rows = dests * lax.axis_size("zh") * CAP
    first = (lax.axis_index("zh") * dests).astype(jnp.int32).reshape(1)
    hbm, vmem = pl.BlockSpec(memory_space=pltpu.HBM), pl.BlockSpec(memory_space=pltpu.VMEM)
    params = pltpu.CompilerParams(vmem_limit_bytes=VMEM)

    with jax.named_scope("tag"):
        own = pl.pallas_call(
            tag_body,
            out_shape=shape(tok_rows, feats + LANES),
            in_specs=[hbm, hbm],
            out_specs=vmem,
            scratch_shapes=[
                pltpu.VMEM((top, tok_rows), jnp.int32),
                pltpu.SemaphoreType.DMA((2,)),
            ],
            compiler_params=params,
        )(in_hbm(tokens), in_hbm(expert_ids.T))
    with jax.named_scope("gather"):
        held = lax.all_gather(own, "zh", tiled=True)
    with jax.named_scope("pack"):
        packed = pl.pallas_call(
            functools.partial(pack_body, tok_rows, top),
            out_shape=pltpu.HBM((rows, feats), BF16),
            in_specs=[pl.BlockSpec(memory_space=pltpu.SMEM), vmem],
            out_specs=hbm,
            scratch_shapes=[
                pltpu.VMEM((rows, feats), BF16),
                pltpu.SemaphoreType.DMA((feats // STEP,)),
            ],
            compiler_params=params,
        )(first, held)
    with jax.named_scope("route"):
        block = lax.all_to_all(
            packed.reshape(dests, -1, feats), near, split_axis=0, concat_axis=0, tiled=True
        )
    routed = block.reshape(rows, feats)
    part_rows = slab // PARTS
    with jax.named_scope("prune"):
        pruned, rest, kept = call(
            prune_body,
            (shape(slab, feats - STEP), shape(slab, STEP), shape(slab, feats)),
            (weight, mask_bits),
            1 << 22,
        )
    with jax.named_scope("project"):
        part, *lows = pl.pallas_call(
            project_body,
            out_shape=(shape(slab, rows, dtype=F32),) + (shape(part_rows, rows),) * PARTS,
            in_specs=[vmem, vmem, hbm],
            out_specs=(vmem,) * (1 + PARTS),
            scratch_shapes=[pltpu.VMEM((slab, STEP), BF16), pltpu.SemaphoreType.DMA],
            cost_estimate=pl.CostEstimate(
                flops=2 * rows * slab * feats, bytes_accessed=1 << 22, transcendentals=0
            ),
            compiler_params=params,
        )(routed, pruned, in_hbm(rest))
    with jax.named_scope("swap_features"):
        others = [shift(low, "yl", 1) for low in lows]
    with jax.named_scope("scale"):
        scale, kept = pl.pallas_call(
            scale_body,
            out_shape=(shape(1, feats, dtype=F32), shape(slab, feats)),
            in_specs=[vmem, vmem, hbm],
            out_specs=(vmem, vmem),
            scratch_shapes=[pltpu.SemaphoreType.DMA],
            compiler_params=params,
        )(routed, damping, in_hbm(kept))
    out = None
    for i, other in enumerate(others):
        operands = (part, other, routed, scale, kept)
        with jax.named_scope("update"):
            out = pl.pallas_call(
                functools.partial(update_body, i * part_rows),
                out_shape=pltpu.HBM((slab, feats), BF16),
                in_specs=[vmem] * len(operands) + [hbm] * (i > 0),
                out_specs=hbm,
                scratch_shapes=[
                    pltpu.VMEM((part_rows, feats), BF16),
                    pltpu.SemaphoreType.DMA((feats // STEP,)),
                ],
                input_output_aliases={len(operands): 0} if i else {},
                cost_estimate=pl.CostEstimate(
                    flops=2 * rows * part_rows * feats,
                    bytes_accessed=1 << 22,
                    transcendentals=0,
                ),
                compiler_params=params,
            )(*operands, *([in_hbm(out)] if i else []))
    return out.reshape(1, slab, feats)


def solution(mesh):
    n_hrow, n_hcol = mesh.shape["hrow"], mesh.shape["hcol"]
    n_expert = mesh.shape["expert"]
    fine = Mesh(
        mesh.devices.reshape(n_expert // 4, 2, 2, n_hrow // 2, 2, n_hcol),
        ("zh", "zl", "yh", "x", "core", "yl"),
    )
    own = ("zh", "zl", "yh", "x", "core")
    in_specs = (P(own, "yl"), P(own, None), P(own, None, "yl"), P(None, "yl"), P(own, "yl"))
    return jax.shard_map(
        local, mesh=fine, in_specs=in_specs, out_specs=P(own, None, "yl"), check_vma=False
    )
```

```python
import functools

import jax
import jax.numpy as jnp
from jax import lax
from jax.experimental import pallas as pl
from jax.experimental.pallas import tpu as pltpu
from jax.sharding import Mesh, PartitionSpec as P

ROWS_E = 128
ETA = 0.5
CAP = 2
LANES = 128
STEP = 512
VMEM = 16 * 2**20
F32 = jnp.float32
BF16 = jnp.bfloat16


def call(body, out_shape, operands, flops, scratch=(), name=None):
    size = sum(o.size * o.dtype.itemsize for o in operands)
    outs = jax.tree.leaves(out_shape)
    size += sum(o.size * o.dtype.itemsize for o in outs)
    return pl.pallas_call(
        body,
        out_shape=out_shape,
        in_specs=[pl.BlockSpec(memory_space=pltpu.VMEM)] * len(operands),
        out_specs=jax.tree.map(lambda _: pl.BlockSpec(memory_space=pltpu.VMEM), out_shape),
        scratch_shapes=list(scratch),
        cost_estimate=pl.CostEstimate(flops=flops, bytes_accessed=size, transcendentals=0),
        compiler_params=pltpu.CompilerParams(vmem_limit_bytes=VMEM),
        name=name,
    )(*operands)


def tag_body(tokens_hbm, ids_hbm, out_ref, ids_ref, sems):
    feats = tokens_hbm.shape[1]
    top = ids_ref.shape[0]
    get_ids = pltpu.make_async_copy(ids_hbm, ids_ref, sems.at[0])
    get_tokens = pltpu.make_async_copy(tokens_hbm, out_ref.at[:, pl.ds(0, feats)], sems.at[1])
    get_ids.start()
    get_tokens.start()
    spread = (
        lax.broadcasted_iota(jnp.int32, (top, LANES), 0)
        == lax.broadcasted_iota(jnp.int32, (top, LANES), 1)
    ).astype(BF16)
    get_ids.wait()
    ids = ids_ref[...].astype(F32).astype(BF16)
    out_ref[:, feats:] = lax.dot_general(
        ids, spread, (((0,), (0,)), ((), ())), preferred_element_type=F32
    ).astype(BF16)
    get_tokens.wait()


def pack_body(tok_rows, top, first_ref, held, out_hbm, out_ref, sems):
    rows, feats = out_ref.shape
    tokens = held.shape[0]
    per_dest = tokens // tok_rows * CAP
    pick = (
        lax.broadcasted_iota(jnp.int32, (top, LANES), 0)
        == lax.broadcasted_iota(jnp.int32, (top, LANES), 1)
    ).astype(BF16)
    ids = lax.dot_general(
        pick, held[:, feats:], (((1,), (1,)), ((), ())), preferred_element_type=F32
    )
    row = lax.broadcasted_iota(jnp.int32, (rows, 1), 0)
    expert = (first_ref[0] + row // per_dest).astype(F32)
    block = (row % per_dest) // CAP
    slot = (row % CAP).astype(F32)
    tok = lax.broadcasted_iota(jnp.int32, (1, tokens), 1)
    named = ids[0:1, :] == expert
    for k in range(1, top):
        named = named | (ids[k : k + 1, :] == expert)
    named = named & (tok // tok_rows == block)
    member = jnp.where(named, 1.0, 0.0)
    before = (
        lax.broadcasted_iota(jnp.int32, (tokens, tokens), 0)
        < lax.broadcasted_iota(jnp.int32, (tokens, tokens), 1)
    ).astype(BF16)
    rank = jnp.dot(member.astype(BF16), before, preferred_element_type=F32)
    select = jnp.where(rank == slot, member, 0.0).astype(BF16)
    copies = []
    for i, lo in enumerate(range(0, feats, STEP)):
        cols = (slice(None), pl.ds(lo, STEP))
        out_ref[cols] = jnp.dot(select, held[cols], preferred_element_type=F32).astype(BF16)
        copies.append(pltpu.make_async_copy(out_ref.at[cols], out_hbm.at[cols], sems.at[i]))
        copies[-1].start()
    for copy in copies:
        copy.wait()


def prune_body(weight_ref, bits_ref, pruned_ref, rest_ref, kept_ref):
    rows, words = bits_ref.shape
    wide = pruned_ref.shape[1]
    lane = lax.broadcasted_iota(jnp.int32, (rows, LANES), 1)
    bits = jnp.concatenate([bits_ref[...], jnp.zeros((rows, LANES - words), jnp.int32)], axis=1)
    for j in range(weight_ref.shape[1] // LANES):
        word = jnp.take_along_axis(bits, lane // 32 + 4 * j, axis=1, mode="promise_in_bounds")
        keep = jnp.bitwise_and(jnp.right_shift(word, lane % 32), 1) == 1
        lo = j * LANES
        slab = weight_ref[:, lo : lo + LANES].astype(F32)
        pruned = jnp.where(keep, 0.0, slab).astype(BF16)
        if lo < wide:
            pruned_ref[:, lo : lo + LANES] = pruned
        else:
            rest_ref[:, lo - wide : lo - wide + LANES] = pruned
        kept_ref[:, lo : lo + LANES] = jnp.where(keep, slab, jnp.inf).astype(BF16)


def project_body(routed_ref, pruned_ref, part_ref):
    part_ref[...] = lax.dot_general(
        pruned_ref[...],
        routed_ref[:, : pruned_ref.shape[1]],
        (((1,), (1,)), ((), ())),
        preferred_element_type=F32,
    )


def finish_body(routed_ref, rest_ref, first_ref, part_ref, low_ref):
    part = first_ref[...] + lax.dot_general(
        rest_ref[...],
        routed_ref[:, routed_ref.shape[1] - rest_ref.shape[1] :],
        (((1,), (1,)), ((), ())),
        preferred_element_type=F32,
    )
    part_ref[...] = part
    low_ref[...] = part.astype(BF16)


def scale_body(routed_ref, damping_ref, kept_hbm, scale_ref, kept_ref, sem):
    fetch = pltpu.make_async_copy(kept_hbm, kept_ref, sem)
    fetch.start()
    feats = damping_ref.shape[1]
    for lo in range(0, feats, STEP):
        cols = slice(lo, lo + STEP)
        rows = routed_ref[:, cols].astype(F32)
        diag = jnp.sum(rows * rows, axis=0, keepdims=True) * (1.0 / ROWS_E) + damping_ref[:, cols]
        scale_ref[:, cols] = (ETA / ROWS_E) / diag
    fetch.wait()


def update_body(part_ref, other_ref, routed_ref, scale_ref, kept_ref, out_hbm, out_ref, sems):
    projected = (part_ref[...] + other_ref[...].astype(F32)).astype(BF16)
    copies = []
    for i, lo in enumerate(range(0, out_ref.shape[1], STEP)):
        cols = slice(lo, lo + STEP)
        comp = jnp.dot(projected, routed_ref[:, cols], preferred_element_type=F32)
        kept = kept_ref[:, cols].astype(F32)
        updated = jnp.where(kept < jnp.inf, kept + comp * scale_ref[:, cols], 0.0)
        out_ref[:, cols] = updated.astype(BF16)
        block = (slice(None), pl.ds(lo, STEP))
        copies.append(pltpu.make_async_copy(out_ref.at[block], out_hbm.at[block], sems.at[i]))
        copies[-1].start()
    for copy in copies:
        copy.wait()


def shape(*dims, dtype=BF16):
    return jax.ShapeDtypeStruct(dims, dtype)


def in_hbm(x):
    return pltpu.with_memory_space_constraint(x, pltpu.HBM)


def shift(x, axis, step):
    n = lax.axis_size(axis)
    return lax.ppermute(x, axis, [(i, (i + step) % n) for i in range(n)])


def local(tokens, expert_ids, weight, mask_bits, damping):
    tok_rows, feats = tokens.shape
    top = expert_ids.shape[1]
    slab = weight.shape[1]
    weight = weight.reshape(slab, feats)
    near = ("zl", "yh", "x", "core")
    dests = lax.axis_size(near)
    n_tok = tok_rows * lax.axis_size("zh")
    rows = dests * lax.axis_size("zh") * CAP
    first = (lax.axis_index("zh") * dests).astype(jnp.int32).reshape(1)
    hbm, vmem = pl.BlockSpec(memory_space=pltpu.HBM), pl.BlockSpec(memory_space=pltpu.VMEM)
    params = pltpu.CompilerParams(vmem_limit_bytes=VMEM)

    with jax.named_scope("tag"):
        own = pl.pallas_call(
            tag_body,
            out_shape=shape(tok_rows, feats + LANES),
            in_specs=[hbm, hbm],
            out_specs=vmem,
            scratch_shapes=[
                pltpu.VMEM((top, tok_rows), jnp.int32),
                pltpu.SemaphoreType.DMA((2,)),
            ],
            compiler_params=params,
        )(in_hbm(tokens), in_hbm(expert_ids.T))
    with jax.named_scope("gather"):
        held = lax.all_gather(own, "zh", tiled=True)
    with jax.named_scope("pack"):
        packed = pl.pallas_call(
            functools.partial(pack_body, tok_rows, top),
            out_shape=pltpu.HBM((rows, feats), BF16),
            in_specs=[pl.BlockSpec(memory_space=pltpu.SMEM), vmem],
            out_specs=hbm,
            scratch_shapes=[
                pltpu.VMEM((rows, feats), BF16),
                pltpu.SemaphoreType.DMA((feats // STEP,)),
            ],
            compiler_params=params,
        )(first, held)
    with jax.named_scope("route"):
        block = lax.all_to_all(
            packed.reshape(dests, -1, feats), near, split_axis=0, concat_axis=0, tiled=True
        )
    routed = block.reshape(rows, feats)
    with jax.named_scope("prune"):
        pruned, rest, kept = call(
            prune_body,
            (shape(slab, feats - STEP), shape(slab, STEP), shape(slab, feats)),
            (weight, mask_bits),
            1 << 22,
        )
    with jax.named_scope("project"):
        most = call(
            project_body,
            shape(slab, rows, dtype=F32),
            (routed, pruned),
            2 * rows * slab * pruned.shape[1],
        )
        part, low = call(
            finish_body,
            (shape(slab, rows, dtype=F32), shape(slab, rows)),
            (routed, rest, most),
            2 * rows * slab * rest.shape[1],
        )
    with jax.named_scope("swap_features"):
        other = shift(low, "yl", 1)
    with jax.named_scope("scale"):
        scale, kept = pl.pallas_call(
            scale_body,
            out_shape=(shape(1, feats, dtype=F32), shape(slab, feats)),
            in_specs=[vmem, vmem, hbm],
            out_specs=(vmem, vmem),
            scratch_shapes=[pltpu.SemaphoreType.DMA],
            compiler_params=params,
        )(routed, damping, in_hbm(kept))
    with jax.named_scope("update"):
        operands = (part, other, routed, scale, kept)
        out = pl.pallas_call(
            update_body,
            out_shape=shape(slab, feats),
            in_specs=[vmem] * len(operands),
            out_specs=hbm,
            scratch_shapes=[
                pltpu.VMEM((slab, feats), BF16),
                pltpu.SemaphoreType.DMA((feats // STEP,)),
            ],
            compiler_params=params,
        )(*operands)
    return out.reshape(1, slab, feats)


def solution(mesh):
    n_hrow, n_hcol = mesh.shape["hrow"], mesh.shape["hcol"]
    n_expert = mesh.shape["expert"]
    fine = Mesh(
        mesh.devices.reshape(n_expert // 4, 2, 2, n_hrow // 2, 2, n_hcol),
        ("zh", "zl", "yh", "x", "core", "yl"),
    )
    own = ("zh", "zl", "yh", "x", "core")
    in_specs = (P(own, "yl"), P(own, None), P(own, None, "yl"), P(None, "yl"), P(own, "yl"))
    return jax.shard_map(
        local, mesh=fine, in_specs=in_specs, out_specs=P(own, None, "yl"), check_vma=False
    )
```

```python
import functools

import jax
import jax.numpy as jnp
from jax import lax
from jax.experimental import pallas as pl
from jax.experimental.pallas import tpu as pltpu
from jax.sharding import Mesh, PartitionSpec as P

ROWS_E = 128
ETA = 0.5
CAP = 2
LANES = 128
STEP = 512
REST = 256
VMEM = 16 * 2**20
F32 = jnp.float32
BF16 = jnp.bfloat16


def call(body, out_shape, operands, flops, scratch=(), name=None):
    size = sum(o.size * o.dtype.itemsize for o in operands)
    outs = jax.tree.leaves(out_shape)
    size += sum(o.size * o.dtype.itemsize for o in outs)
    return pl.pallas_call(
        body,
        out_shape=out_shape,
        in_specs=[pl.BlockSpec(memory_space=pltpu.VMEM)] * len(operands),
        out_specs=jax.tree.map(lambda _: pl.BlockSpec(memory_space=pltpu.VMEM), out_shape),
        scratch_shapes=list(scratch),
        cost_estimate=pl.CostEstimate(flops=flops, bytes_accessed=size, transcendentals=0),
        compiler_params=pltpu.CompilerParams(vmem_limit_bytes=VMEM),
        name=name,
    )(*operands)


def tag_body(tokens_hbm, ids_hbm, out_ref, ids_ref, sems):
    feats = tokens_hbm.shape[1]
    top = ids_ref.shape[0]
    get_ids = pltpu.make_async_copy(ids_hbm, ids_ref, sems.at[0])
    get_tokens = pltpu.make_async_copy(tokens_hbm, out_ref.at[:, pl.ds(0, feats)], sems.at[1])
    get_ids.start()
    get_tokens.start()
    spread = (
        lax.broadcasted_iota(jnp.int32, (top, LANES), 0)
        == lax.broadcasted_iota(jnp.int32, (top, LANES), 1)
    ).astype(BF16)
    get_ids.wait()
    ids = ids_ref[...].astype(F32).astype(BF16)
    out_ref[:, feats:] = lax.dot_general(
        ids, spread, (((0,), (0,)), ((), ())), preferred_element_type=F32
    ).astype(BF16)
    get_tokens.wait()


def pack_body(tok_rows, top, first_ref, held, out_hbm, out_ref, sems):
    rows, feats = out_ref.shape
    tokens = held.shape[0]
    per_dest = tokens // tok_rows * CAP
    pick = (
        lax.broadcasted_iota(jnp.int32, (top, LANES), 0)
        == lax.broadcasted_iota(jnp.int32, (top, LANES), 1)
    ).astype(BF16)
    ids = lax.dot_general(
        pick, held[:, feats:], (((1,), (1,)), ((), ())), preferred_element_type=F32
    )
    row = lax.broadcasted_iota(jnp.int32, (rows, 1), 0)
    expert = (first_ref[0] + row // per_dest).astype(F32)
    block = (row % per_dest) // CAP
    slot = (row % CAP).astype(F32)
    tok = lax.broadcasted_iota(jnp.int32, (1, tokens), 1)
    named = ids[0:1, :] == expert
    for k in range(1, top):
        named = named | (ids[k : k + 1, :] == expert)
    named = named & (tok // tok_rows == block)
    member = jnp.where(named, 1.0, 0.0)
    before = (
        lax.broadcasted_iota(jnp.int32, (tokens, tokens), 0)
        < lax.broadcasted_iota(jnp.int32, (tokens, tokens), 1)
    ).astype(BF16)
    rank = jnp.dot(member.astype(BF16), before, preferred_element_type=F32)
    select = jnp.where(rank == slot, member, 0.0).astype(BF16)
    copies = []
    for i, lo in enumerate(range(0, feats, STEP)):
        cols = (slice(None), pl.ds(lo, STEP))
        out_ref[cols] = jnp.dot(select, held[cols], preferred_element_type=F32).astype(BF16)
        copies.append(pltpu.make_async_copy(out_ref.at[cols], out_hbm.at[cols], sems.at[i]))
        copies[-1].start()
    for copy in copies:
        copy.wait()


def prune_body(weight_ref, bits_ref, pruned_ref, rest_ref, kept_ref):
    rows, words = bits_ref.shape
    wide = pruned_ref.shape[1]
    lane = lax.broadcasted_iota(jnp.int32, (rows, LANES), 1)
    bits = jnp.concatenate([bits_ref[...], jnp.zeros((rows, LANES - words), jnp.int32)], axis=1)
    for j in range(weight_ref.shape[1] // LANES):
        word = jnp.take_along_axis(bits, lane // 32 + 4 * j, axis=1, mode="promise_in_bounds")
        keep = jnp.bitwise_and(jnp.right_shift(word, lane % 32), 1) == 1
        lo = j * LANES
        slab = weight_ref[:, lo : lo + LANES].astype(F32)
        pruned = jnp.where(keep, 0.0, slab).astype(BF16)
        if lo < wide:
            pruned_ref[:, lo : lo + LANES] = pruned
        else:
            rest_ref[:, lo - wide : lo - wide + LANES] = pruned
        kept_ref[:, lo : lo + LANES] = jnp.where(keep, slab, jnp.inf).astype(BF16)


def project_body(routed_ref, pruned_ref, part_ref):
    part_ref[...] = lax.dot_general(
        pruned_ref[...],
        routed_ref[:, : pruned_ref.shape[1]],
        (((1,), (1,)), ((), ())),
        preferred_element_type=F32,
    )


def finish_body(routed_ref, rest_ref, first_ref, part_ref, low_ref):
    part = first_ref[...] + lax.dot_general(
        rest_ref[...],
        routed_ref[:, routed_ref.shape[1] - rest_ref.shape[1] :],
        (((1,), (1,)), ((), ())),
        preferred_element_type=F32,
    )
    part_ref[...] = part
    low_ref[...] = part.astype(BF16)


def scale_body(routed_ref, damping_ref, kept_hbm, scale_ref, kept_ref, sem):
    fetch = pltpu.make_async_copy(kept_hbm, kept_ref, sem)
    fetch.start()
    feats = damping_ref.shape[1]
    for lo in range(0, feats, STEP):
        cols = slice(lo, lo + STEP)
        rows = routed_ref[:, cols].astype(F32)
        diag = jnp.sum(rows * rows, axis=0, keepdims=True) * (1.0 / ROWS_E) + damping_ref[:, cols]
        scale_ref[:, cols] = (ETA / ROWS_E) / diag
    fetch.wait()


def update_body(part_ref, other_ref, routed_ref, scale_ref, kept_ref, out_hbm, out_ref, sems):
    projected = (part_ref[...] + other_ref[...].astype(F32)).astype(BF16)
    copies = []
    for i, lo in enumerate(range(0, out_ref.shape[1], STEP)):
        cols = slice(lo, lo + STEP)
        comp = jnp.dot(projected, routed_ref[:, cols], preferred_element_type=F32)
        kept = kept_ref[:, cols]
        updated = (kept.astype(F32) + comp * scale_ref[:, cols]).astype(BF16)
        out_ref[:, cols] = jnp.where(kept < jnp.inf, updated, jnp.zeros_like(updated))
        block = (slice(None), pl.ds(lo, STEP))
        copies.append(pltpu.make_async_copy(out_ref.at[block], out_hbm.at[block], sems.at[i]))
        copies[-1].start()
    for copy in copies:
        copy.wait()


def shape(*dims, dtype=BF16):
    return jax.ShapeDtypeStruct(dims, dtype)


def in_hbm(x):
    return pltpu.with_memory_space_constraint(x, pltpu.HBM)


def shift(x, axis, step):
    n = lax.axis_size(axis)
    return lax.ppermute(x, axis, [(i, (i + step) % n) for i in range(n)])


def local(tokens, expert_ids, weight, mask_bits, damping):
    tok_rows, feats = tokens.shape
    top = expert_ids.shape[1]
    slab = weight.shape[1]
    weight = weight.reshape(slab, feats)
    near = ("zl", "yh", "x", "core")
    dests = lax.axis_size(near)
    n_tok = tok_rows * lax.axis_size("zh")
    rows = dests * lax.axis_size("zh") * CAP
    first = (lax.axis_index("zh") * dests).astype(jnp.int32).reshape(1)
    hbm, vmem = pl.BlockSpec(memory_space=pltpu.HBM), pl.BlockSpec(memory_space=pltpu.VMEM)
    params = pltpu.CompilerParams(vmem_limit_bytes=VMEM)

    with jax.named_scope("tag"):
        own = pl.pallas_call(
            tag_body,
            out_shape=shape(tok_rows, feats + LANES),
            in_specs=[hbm, hbm],
            out_specs=vmem,
            scratch_shapes=[
                pltpu.VMEM((top, tok_rows), jnp.int32),
                pltpu.SemaphoreType.DMA((2,)),
            ],
            compiler_params=params,
        )(in_hbm(tokens), in_hbm(expert_ids.T))
    with jax.named_scope("gather"):
        held = lax.all_gather(own, "zh", tiled=True)
    with jax.named_scope("pack"):
        packed = pl.pallas_call(
            functools.partial(pack_body, tok_rows, top),
            out_shape=pltpu.HBM((rows, feats), BF16),
            in_specs=[pl.BlockSpec(memory_space=pltpu.SMEM), vmem],
            out_specs=hbm,
            scratch_shapes=[
                pltpu.VMEM((rows, feats), BF16),
                pltpu.SemaphoreType.DMA((feats // STEP,)),
            ],
            compiler_params=params,
        )(first, held)
    with jax.named_scope("route"):
        block = lax.all_to_all(
            packed.reshape(dests, -1, feats), near, split_axis=0, concat_axis=0, tiled=True
        )
    routed = block.reshape(rows, feats)
    with jax.named_scope("prune"):
        pruned, rest, kept = call(
            prune_body,
            (shape(slab, feats - REST), shape(slab, REST), shape(slab, feats)),
            (weight, mask_bits),
            1 << 22,
        )
    with jax.named_scope("project"):
        most = call(
            project_body,
            shape(slab, rows, dtype=F32),
            (routed, pruned),
            2 * rows * slab * pruned.shape[1],
        )
        part, low = call(
            finish_body,
            (shape(slab, rows, dtype=F32), shape(slab, rows)),
            (routed, rest, most),
            2 * rows * slab * rest.shape[1],
        )
    with jax.named_scope("swap_features"):
        other = shift(low, "yl", 1)
    with jax.named_scope("scale"):
        scale, kept = pl.pallas_call(
            scale_body,
            out_shape=(shape(1, feats, dtype=F32), shape(slab, feats)),
            in_specs=[vmem, vmem, hbm],
            out_specs=(vmem, vmem),
            scratch_shapes=[pltpu.SemaphoreType.DMA],
            compiler_params=params,
        )(routed, damping, in_hbm(kept))
    with jax.named_scope("update"):
        operands = (part, other, routed, scale, kept)
        out = pl.pallas_call(
            update_body,
            out_shape=shape(slab, feats),
            in_specs=[vmem] * len(operands),
            out_specs=hbm,
            scratch_shapes=[
                pltpu.VMEM((slab, feats), BF16),
                pltpu.SemaphoreType.DMA((feats // STEP,)),
            ],
            compiler_params=params,
        )(*operands)
    return out.reshape(1, slab, feats)


def solution(mesh):
    n_hrow, n_hcol = mesh.shape["hrow"], mesh.shape["hcol"]
    n_expert = mesh.shape["expert"]
    fine = Mesh(
        mesh.devices.reshape(n_expert // 4, 2, 2, n_hrow // 2, 2, n_hcol),
        ("zh", "zl", "yh", "x", "core", "yl"),
    )
    own = ("zh", "zl", "yh", "x", "core")
    in_specs = (P(own, "yl"), P(own, None), P(own, None, "yl"), P(None, "yl"), P(own, "yl"))
    return jax.shard_map(
        local, mesh=fine, in_specs=in_specs, out_specs=P(own, None, "yl"), check_vma=False
    )
```

```python
import functools

import jax
import jax.numpy as jnp
from jax import lax
from jax.experimental import pallas as pl
from jax.experimental.pallas import tpu as pltpu
from jax.sharding import Mesh, PartitionSpec as P

ROWS_E = 128
ETA = 0.5
CAP = 2
LANES = 128
STEP = 512
REST = 256
VMEM = 16 * 2**20
F32 = jnp.float32
BF16 = jnp.bfloat16


def call(body, out_shape, operands, flops, scratch=(), name=None):
    size = sum(o.size * o.dtype.itemsize for o in operands)
    outs = jax.tree.leaves(out_shape)
    size += sum(o.size * o.dtype.itemsize for o in outs)
    return pl.pallas_call(
        body,
        out_shape=out_shape,
        in_specs=[pl.BlockSpec(memory_space=pltpu.VMEM)] * len(operands),
        out_specs=jax.tree.map(lambda _: pl.BlockSpec(memory_space=pltpu.VMEM), out_shape),
        scratch_shapes=list(scratch),
        cost_estimate=pl.CostEstimate(flops=flops, bytes_accessed=size, transcendentals=0),
        compiler_params=pltpu.CompilerParams(vmem_limit_bytes=VMEM),
        name=name,
    )(*operands)


def tag_body(tokens_hbm, ids_hbm, out_ref, ids_ref, sems):
    feats = tokens_hbm.shape[1]
    top = ids_ref.shape[0]
    get_ids = pltpu.make_async_copy(ids_hbm, ids_ref, sems.at[0])
    get_tokens = pltpu.make_async_copy(tokens_hbm, out_ref.at[:, pl.ds(0, feats)], sems.at[1])
    get_ids.start()
    get_tokens.start()
    spread = (
        lax.broadcasted_iota(jnp.int32, (top, LANES), 0)
        == lax.broadcasted_iota(jnp.int32, (top, LANES), 1)
    ).astype(BF16)
    rows = out_ref.shape[0]
    earlier = (
        lax.broadcasted_iota(jnp.int32, (rows, rows), 1)
        < lax.broadcasted_iota(jnp.int32, (rows, rows), 0)
    ).astype(BF16)
    expert = lax.broadcasted_iota(jnp.int32, (rows, LANES), 1).astype(F32)
    get_ids.wait()
    ids = lax.dot_general(
        ids_ref[...].astype(F32).astype(BF16),
        spread,
        (((0,), (0,)), ((), ())),
        preferred_element_type=F32,
    )
    named = ids[:, 0:1] == expert
    for k in range(1, top):
        named = named | (ids[:, k : k + 1] == expert)
    member = jnp.where(named, 1.0, 0.0)
    rank = jnp.dot(earlier, member.astype(BF16), preferred_element_type=F32)
    out_ref[:, feats:] = (member * (1.0 + rank)).astype(BF16)
    get_tokens.wait()


def pack_body(tok_rows, first_ref, held, out_hbm, out_ref, sems):
    rows, feats = out_ref.shape
    tokens = held.shape[0]
    per_dest = tokens // tok_rows * CAP
    row = lax.broadcasted_iota(jnp.int32, (rows, 1), 0)
    expert = first_ref[0] + row // per_dest
    pick = (lax.broadcasted_iota(jnp.int32, (rows, LANES), 1) == expert).astype(BF16)
    taken = lax.dot_general(
        pick, held[:, feats:], (((1,), (1,)), ((), ())), preferred_element_type=F32
    )
    block = (row % per_dest) // CAP
    slot = (row % CAP).astype(F32)
    tok = lax.broadcasted_iota(jnp.int32, (1, tokens), 1)
    mine = (tok // tok_rows == block) & (taken == slot + 1.0)
    select = jnp.where(mine, 1.0, 0.0).astype(BF16)
    copies = []
    for i, lo in enumerate(range(0, feats, STEP)):
        cols = (slice(None), pl.ds(lo, STEP))
        out_ref[cols] = jnp.dot(select, held[cols], preferred_element_type=F32).astype(BF16)
        copies.append(pltpu.make_async_copy(out_ref.at[cols], out_hbm.at[cols], sems.at[i]))
        copies[-1].start()
    for copy in copies:
        copy.wait()


def prune_body(weight_ref, bits_ref, pruned_ref, rest_ref, kept_ref):
    rows, words = bits_ref.shape
    wide = pruned_ref.shape[1]
    lane = lax.broadcasted_iota(jnp.int32, (rows, LANES), 1)
    bits = jnp.concatenate([bits_ref[...], jnp.zeros((rows, LANES - words), jnp.int32)], axis=1)
    for j in range(weight_ref.shape[1] // LANES):
        word = jnp.take_along_axis(bits, lane // 32 + 4 * j, axis=1, mode="promise_in_bounds")
        keep = jnp.bitwise_and(jnp.right_shift(word, lane % 32), 1) == 1
        lo = j * LANES
        slab = weight_ref[:, lo : lo + LANES].astype(F32)
        pruned = jnp.where(keep, 0.0, slab).astype(BF16)
        if lo < wide:
            pruned_ref[:, lo : lo + LANES] = pruned
        else:
            rest_ref[:, lo - wide : lo - wide + LANES] = pruned
        kept_ref[:, lo : lo + LANES] = jnp.where(keep, slab, jnp.inf).astype(BF16)


def project_body(routed_ref, pruned_ref, part_ref):
    part_ref[...] = lax.dot_general(
        pruned_ref[...],
        routed_ref[:, : pruned_ref.shape[1]],
        (((1,), (1,)), ((), ())),
        preferred_element_type=F32,
    )


def finish_body(routed_ref, rest_ref, first_ref, part_ref, low_ref):
    part = first_ref[...] + lax.dot_general(
        rest_ref[...],
        routed_ref[:, routed_ref.shape[1] - rest_ref.shape[1] :],
        (((1,), (1,)), ((), ())),
        preferred_element_type=F32,
    )
    part_ref[...] = part
    low_ref[...] = part.astype(BF16)


def scale_body(routed_ref, damping_ref, kept_hbm, scale_ref, kept_ref, sem):
    fetch = pltpu.make_async_copy(kept_hbm, kept_ref, sem)
    fetch.start()
    feats = damping_ref.shape[1]
    for lo in range(0, feats, STEP):
        cols = slice(lo, lo + STEP)
        rows = routed_ref[:, cols].astype(F32)
        diag = jnp.sum(rows * rows, axis=0, keepdims=True) * (1.0 / ROWS_E) + damping_ref[:, cols]
        scale_ref[:, cols] = (ETA / ROWS_E) / diag
    fetch.wait()


def update_body(part_ref, other_ref, routed_ref, scale_ref, kept_ref, out_hbm, out_ref, sems):
    projected = (part_ref[...] + other_ref[...].astype(F32)).astype(BF16)
    copies = []
    for i, lo in enumerate(range(0, out_ref.shape[1], STEP)):
        cols = slice(lo, lo + STEP)
        comp = jnp.dot(projected, routed_ref[:, cols], preferred_element_type=F32)
        kept = kept_ref[:, cols]
        updated = (kept.astype(F32) + comp * scale_ref[:, cols]).astype(BF16)
        out_ref[:, cols] = jnp.where(kept < jnp.inf, updated, jnp.zeros_like(updated))
        block = (slice(None), pl.ds(lo, STEP))
        copies.append(pltpu.make_async_copy(out_ref.at[block], out_hbm.at[block], sems.at[i]))
        copies[-1].start()
    for copy in copies:
        copy.wait()


def shape(*dims, dtype=BF16):
    return jax.ShapeDtypeStruct(dims, dtype)


def in_hbm(x):
    return pltpu.with_memory_space_constraint(x, pltpu.HBM)


def shift(x, axis, step):
    n = lax.axis_size(axis)
    return lax.ppermute(x, axis, [(i, (i + step) % n) for i in range(n)])


def local(tokens, expert_ids, weight, mask_bits, damping):
    tok_rows, feats = tokens.shape
    top = expert_ids.shape[1]
    slab = weight.shape[1]
    weight = weight.reshape(slab, feats)
    near = ("zl", "yh", "x", "core")
    dests = lax.axis_size(near)
    n_tok = tok_rows * lax.axis_size("zh")
    rows = dests * lax.axis_size("zh") * CAP
    first = (lax.axis_index("zh") * dests).astype(jnp.int32).reshape(1)
    hbm, vmem = pl.BlockSpec(memory_space=pltpu.HBM), pl.BlockSpec(memory_space=pltpu.VMEM)
    params = pltpu.CompilerParams(vmem_limit_bytes=VMEM)

    with jax.named_scope("tag"):
        own = pl.pallas_call(
            tag_body,
            out_shape=shape(tok_rows, feats + LANES),
            in_specs=[hbm, hbm],
            out_specs=vmem,
            scratch_shapes=[
                pltpu.VMEM((top, tok_rows), jnp.int32),
                pltpu.SemaphoreType.DMA((2,)),
            ],
            compiler_params=params,
        )(in_hbm(tokens), in_hbm(expert_ids.T))
    with jax.named_scope("gather"):
        held = lax.all_gather(own, "zh", tiled=True)
    with jax.named_scope("pack"):
        packed = pl.pallas_call(
            functools.partial(pack_body, tok_rows),
            out_shape=pltpu.HBM((rows, feats), BF16),
            in_specs=[pl.BlockSpec(memory_space=pltpu.SMEM), vmem],
            out_specs=hbm,
            scratch_shapes=[
                pltpu.VMEM((rows, feats), BF16),
                pltpu.SemaphoreType.DMA((feats // STEP,)),
            ],
            compiler_params=params,
        )(first, held)
    with jax.named_scope("route"):
        block = lax.all_to_all(
            packed.reshape(dests, -1, feats), near, split_axis=0, concat_axis=0, tiled=True
        )
    routed = block.reshape(rows, feats)
    with jax.named_scope("prune"):
        pruned, rest, kept = call(
            prune_body,
            (shape(slab, feats - REST), shape(slab, REST), shape(slab, feats)),
            (weight, mask_bits),
            1 << 22,
        )
    with jax.named_scope("project"):
        most = call(
            project_body,
            shape(slab, rows, dtype=F32),
            (routed, pruned),
            2 * rows * slab * pruned.shape[1],
        )
        part, low = call(
            finish_body,
            (shape(slab, rows, dtype=F32), shape(slab, rows)),
            (routed, rest, most),
            2 * rows * slab * rest.shape[1],
        )
    with jax.named_scope("swap_features"):
        other = shift(low, "yl", 1)
    with jax.named_scope("scale"):
        scale, kept = pl.pallas_call(
            scale_body,
            out_shape=(shape(1, feats, dtype=F32), shape(slab, feats)),
            in_specs=[vmem, vmem, hbm],
            out_specs=(vmem, vmem),
            scratch_shapes=[pltpu.SemaphoreType.DMA],
            compiler_params=params,
        )(routed, damping, in_hbm(kept))
    with jax.named_scope("update"):
        operands = (part, other, routed, scale, kept)
        out = pl.pallas_call(
            update_body,
            out_shape=shape(slab, feats),
            in_specs=[vmem] * len(operands),
            out_specs=hbm,
            scratch_shapes=[
                pltpu.VMEM((slab, feats), BF16),
                pltpu.SemaphoreType.DMA((feats // STEP,)),
            ],
            compiler_params=params,
        )(*operands)
    return out.reshape(1, slab, feats)


def solution(mesh):
    n_hrow, n_hcol = mesh.shape["hrow"], mesh.shape["hcol"]
    n_expert = mesh.shape["expert"]
    fine = Mesh(
        mesh.devices.reshape(n_expert // 4, 2, 2, n_hrow // 2, 2, n_hcol),
        ("zh", "zl", "yh", "x", "core", "yl"),
    )
    own = ("zh", "zl", "yh", "x", "core")
    in_specs = (P(own, "yl"), P(own, None), P(own, None, "yl"), P(None, "yl"), P(own, "yl"))
    return jax.shard_map(
        local, mesh=fine, in_specs=in_specs, out_specs=P(own, None, "yl"), check_vma=False
    )
```

```python
import functools

import jax
import jax.numpy as jnp
from jax import lax
from jax.experimental import pallas as pl
from jax.experimental.pallas import tpu as pltpu
from jax.sharding import Mesh, PartitionSpec as P

ROWS_E = 128
ETA = 0.5
CAP = 2
LANES = 128
STEP = 512
FINE = 256
REST = 256
VMEM = 16 * 2**20
F32 = jnp.float32
BF16 = jnp.bfloat16


def call(body, out_shape, operands, flops, scratch=(), name=None):
    size = sum(o.size * o.dtype.itemsize for o in operands)
    outs = jax.tree.leaves(out_shape)
    size += sum(o.size * o.dtype.itemsize for o in outs)
    return pl.pallas_call(
        body,
        out_shape=out_shape,
        in_specs=[pl.BlockSpec(memory_space=pltpu.VMEM)] * len(operands),
        out_specs=jax.tree.map(lambda _: pl.BlockSpec(memory_space=pltpu.VMEM), out_shape),
        scratch_shapes=list(scratch),
        cost_estimate=pl.CostEstimate(flops=flops, bytes_accessed=size, transcendentals=0),
        compiler_params=pltpu.CompilerParams(vmem_limit_bytes=VMEM),
        name=name,
    )(*operands)


def tag_body(tokens_hbm, ids_hbm, out_ref, ids_ref, sems):
    feats = tokens_hbm.shape[1]
    top = ids_ref.shape[0]
    get_ids = pltpu.make_async_copy(ids_hbm, ids_ref, sems.at[0])
    get_tokens = pltpu.make_async_copy(tokens_hbm, out_ref.at[:, pl.ds(0, feats)], sems.at[1])
    get_ids.start()
    get_tokens.start()
    spread = (
        lax.broadcasted_iota(jnp.int32, (top, LANES), 0)
        == lax.broadcasted_iota(jnp.int32, (top, LANES), 1)
    ).astype(BF16)
    rows = out_ref.shape[0]
    earlier = (
        lax.broadcasted_iota(jnp.int32, (rows, rows), 1)
        < lax.broadcasted_iota(jnp.int32, (rows, rows), 0)
    ).astype(BF16)
    expert = lax.broadcasted_iota(jnp.int32, (rows, LANES), 1).astype(F32)
    get_ids.wait()
    ids = lax.dot_general(
        ids_ref[...].astype(F32).astype(BF16),
        spread,
        (((0,), (0,)), ((), ())),
        preferred_element_type=F32,
    )
    named = ids[:, 0:1] == expert
    for k in range(1, top):
        named = named | (ids[:, k : k + 1] == expert)
    member = jnp.where(named, 1.0, 0.0)
    rank = jnp.dot(earlier, member.astype(BF16), preferred_element_type=F32)
    out_ref[:, feats:] = (member * (1.0 + rank)).astype(BF16)
    get_tokens.wait()


def pack_body(tok_rows, first_ref, held, out_hbm, out_ref, sems):
    rows, feats = out_ref.shape
    tokens = held.shape[0]
    per_dest = tokens // tok_rows * CAP
    row = lax.broadcasted_iota(jnp.int32, (rows, 1), 0)
    expert = first_ref[0] + row // per_dest
    pick = (lax.broadcasted_iota(jnp.int32, (rows, LANES), 1) == expert).astype(BF16)
    taken = lax.dot_general(
        pick, held[:, feats:], (((1,), (1,)), ((), ())), preferred_element_type=F32
    )
    block = (row % per_dest) // CAP
    slot = (row % CAP).astype(F32)
    tok = lax.broadcasted_iota(jnp.int32, (1, tokens), 1)
    mine = (tok // tok_rows == block) & (taken == slot + 1.0)
    select = jnp.where(mine, 1.0, 0.0).astype(BF16)
    copies = []
    for i, lo in enumerate(range(0, feats, STEP)):
        cols = (slice(None), pl.ds(lo, STEP))
        out_ref[cols] = jnp.dot(select, held[cols], preferred_element_type=F32).astype(BF16)
        copies.append(pltpu.make_async_copy(out_ref.at[cols], out_hbm.at[cols], sems.at[i]))
        copies[-1].start()
    for copy in copies:
        copy.wait()


def prune_body(weight_ref, bits_ref, pruned_ref, rest_ref, kept_ref):
    rows, words = bits_ref.shape
    wide = pruned_ref.shape[1]
    lane = lax.broadcasted_iota(jnp.int32, (rows, LANES), 1)
    bits = jnp.concatenate([bits_ref[...], jnp.zeros((rows, LANES - words), jnp.int32)], axis=1)
    for j in range(weight_ref.shape[1] // LANES):
        word = jnp.take_along_axis(bits, lane // 32 + 4 * j, axis=1, mode="promise_in_bounds")
        keep = jnp.bitwise_and(jnp.right_shift(word, lane % 32), 1) == 1
        lo = j * LANES
        slab = weight_ref[:, lo : lo + LANES].astype(F32)
        pruned = jnp.where(keep, 0.0, slab).astype(BF16)
        if lo < wide:
            pruned_ref[:, lo : lo + LANES] = pruned
        else:
            rest_ref[:, lo - wide : lo - wide + LANES] = pruned
        kept_ref[:, lo : lo + LANES] = jnp.where(keep, slab, jnp.inf).astype(BF16)


def project_body(routed_ref, pruned_ref, part_ref):
    part_ref[...] = lax.dot_general(
        pruned_ref[...],
        routed_ref[:, : pruned_ref.shape[1]],
        (((1,), (1,)), ((), ())),
        preferred_element_type=F32,
    )


def finish_body(routed_ref, rest_ref, first_ref, part_ref, low_ref):
    part = first_ref[...] + lax.dot_general(
        rest_ref[...],
        routed_ref[:, routed_ref.shape[1] - rest_ref.shape[1] :],
        (((1,), (1,)), ((), ())),
        preferred_element_type=F32,
    )
    part_ref[...] = part
    low_ref[...] = part.astype(BF16)


def scale_body(routed_ref, damping_ref, kept_hbm, scale_ref, kept_ref, sem):
    fetch = pltpu.make_async_copy(kept_hbm, kept_ref, sem)
    fetch.start()
    feats = damping_ref.shape[1]
    for lo in range(0, feats, STEP):
        cols = slice(lo, lo + STEP)
        rows = routed_ref[:, cols].astype(F32)
        diag = jnp.sum(rows * rows, axis=0, keepdims=True) * (1.0 / ROWS_E) + damping_ref[:, cols]
        scale_ref[:, cols] = (ETA / ROWS_E) / diag
    fetch.wait()


def update_body(part_ref, other_ref, routed_ref, scale_ref, kept_ref, out_hbm, out_ref, sems):
    projected = (part_ref[...] + other_ref[...].astype(F32)).astype(BF16)
    copies = []
    for i, lo in enumerate(range(0, out_ref.shape[1], FINE)):
        cols = slice(lo, lo + FINE)
        comp = jnp.dot(projected, routed_ref[:, cols], preferred_element_type=F32)
        kept = kept_ref[:, cols]
        updated = (kept.astype(F32) + comp * scale_ref[:, cols]).astype(BF16)
        out_ref[:, cols] = jnp.where(kept < jnp.inf, updated, jnp.zeros_like(updated))
        block = (slice(None), pl.ds(lo, FINE))
        copies.append(pltpu.make_async_copy(out_ref.at[block], out_hbm.at[block], sems.at[i]))
        copies[-1].start()
    for copy in copies:
        copy.wait()


def shape(*dims, dtype=BF16):
    return jax.ShapeDtypeStruct(dims, dtype)


def in_hbm(x):
    return pltpu.with_memory_space_constraint(x, pltpu.HBM)


def shift(x, axis, step):
    n = lax.axis_size(axis)
    return lax.ppermute(x, axis, [(i, (i + step) % n) for i in range(n)])


def local(tokens, expert_ids, weight, mask_bits, damping):
    tok_rows, feats = tokens.shape
    top = expert_ids.shape[1]
    slab = weight.shape[1]
    weight = weight.reshape(slab, feats)
    near = ("zl", "yh", "x", "core")
    dests = lax.axis_size(near)
    n_tok = tok_rows * lax.axis_size("zh")
    rows = dests * lax.axis_size("zh") * CAP
    first = (lax.axis_index("zh") * dests).astype(jnp.int32).reshape(1)
    hbm, vmem = pl.BlockSpec(memory_space=pltpu.HBM), pl.BlockSpec(memory_space=pltpu.VMEM)
    params = pltpu.CompilerParams(vmem_limit_bytes=VMEM)

    with jax.named_scope("tag"):
        own = pl.pallas_call(
            tag_body,
            out_shape=shape(tok_rows, feats + LANES),
            in_specs=[hbm, hbm],
            out_specs=vmem,
            scratch_shapes=[
                pltpu.VMEM((top, tok_rows), jnp.int32),
                pltpu.SemaphoreType.DMA((2,)),
            ],
            compiler_params=params,
        )(in_hbm(tokens), in_hbm(expert_ids.T))
    with jax.named_scope("gather"):
        held = lax.all_gather(own, "zh", tiled=True)
    with jax.named_scope("pack"):
        packed = pl.pallas_call(
            functools.partial(pack_body, tok_rows),
            out_shape=pltpu.HBM((rows, feats), BF16),
            in_specs=[pl.BlockSpec(memory_space=pltpu.SMEM), vmem],
            out_specs=hbm,
            scratch_shapes=[
                pltpu.VMEM((rows, feats), BF16),
                pltpu.SemaphoreType.DMA((feats // STEP,)),
            ],
            compiler_params=params,
        )(first, held)
    with jax.named_scope("route"):
        block = lax.all_to_all(
            packed.reshape(dests, -1, feats), near, split_axis=0, concat_axis=0, tiled=True
        )
    routed = block.reshape(rows, feats)
    with jax.named_scope("prune"):
        pruned, rest, kept = call(
            prune_body,
            (shape(slab, feats - REST), shape(slab, REST), shape(slab, feats)),
            (weight, mask_bits),
            1 << 22,
        )
    with jax.named_scope("project"):
        most = call(
            project_body,
            shape(slab, rows, dtype=F32),
            (routed, pruned),
            2 * rows * slab * pruned.shape[1],
        )
        part, low = call(
            finish_body,
            (shape(slab, rows, dtype=F32), shape(slab, rows)),
            (routed, rest, most),
            2 * rows * slab * rest.shape[1],
        )
    with jax.named_scope("swap_features"):
        other = shift(low, "yl", 1)
    with jax.named_scope("scale"):
        scale, kept = pl.pallas_call(
            scale_body,
            out_shape=(shape(1, feats, dtype=F32), shape(slab, feats)),
            in_specs=[vmem, vmem, hbm],
            out_specs=(vmem, vmem),
            scratch_shapes=[pltpu.SemaphoreType.DMA],
            compiler_params=params,
        )(routed, damping, in_hbm(kept))
    with jax.named_scope("update"):
        operands = (part, other, routed, scale, kept)
        out = pl.pallas_call(
            update_body,
            out_shape=shape(slab, feats),
            in_specs=[vmem] * len(operands),
            out_specs=hbm,
            scratch_shapes=[
                pltpu.VMEM((slab, feats), BF16),
                pltpu.SemaphoreType.DMA((feats // FINE,)),
            ],
            compiler_params=params,
        )(*operands)
    return out.reshape(1, slab, feats)


def solution(mesh):
    n_hrow, n_hcol = mesh.shape["hrow"], mesh.shape["hcol"]
    n_expert = mesh.shape["expert"]
    fine = Mesh(
        mesh.devices.reshape(n_expert // 4, 2, 2, n_hrow // 2, 2, n_hcol),
        ("zh", "zl", "yh", "x", "core", "yl"),
    )
    own = ("zh", "zl", "yh", "x", "core")
    in_specs = (P(own, "yl"), P(own, None), P(own, None, "yl"), P(None, "yl"), P(own, "yl"))
    return jax.shard_map(
        local, mesh=fine, in_specs=in_specs, out_specs=P(own, None, "yl"), check_vma=False
    )
```
